256 devices in a mesh: gz: 64 (over x_lo, y, z), col: 4 (over x_hi, core).
Axes of the slice: x: 4 (x_hi: 2, x_lo: 2; x = x_hi * 2 + x_lo), y: 4, z: 8, core: 2. Of those that a mesh axis runs over, the one named last changes fastest.
Arguments:
- x_field: bfloat16 [64, 128, 1024], P('gz', 'col'), may hold values from -40 to 40
- weights: bfloat16 [256, 3456], P('col'), may hold values from -0.109375 to 0.109375
- grad_out: bfloat16 [64, 256, 1024], P('gz', 'col'), may hold values from -40 to 40
Outputs:
- y_field: bfloat16 [64, 256, 1024], P('gz', 'col')
- grad_input: bfloat16 [64, 128, 1024], P('gz', 'col')
- grad_weights: float32 [3456, 256], P('gz', 'col')
- patch_factor: float32 [3456, 3456], P('gz', 'col')
- grad_factor: float32 [256, 256], P('gz', 'col')
The draws below stay inside these ranges and needn't reach their ends.
All inputs are finite; a program needn't handle non-finite values.
Results may differ from the reference program's by a relative error of at most 0.0008.
Values may be sent and summed in bfloat16 or wider, within the bound.
A program may use at most 384 MiB of HBM per device.

```python
import math
import jax
import jax.numpy as jnp
from jax import lax

CIN = 128
COUT = 256
TAPS = 27
S = 32
YX = 1024
KDIM = 3456
NZ = 64


def scaled_field(key, channels):
    key_base, key_chan = jax.random.split(key)
    shape = (NZ, channels, YX)
    zpos = jnp.arange(NZ, dtype=jnp.float32) / max(NZ - 1, 1)
    zscale = 0.6 * jnp.exp(zpos * math.log(3.0))
    chan = jnp.exp(jax.random.uniform(key_chan, (channels,), jnp.float32, math.log(0.3), math.log(3.0)))
    base = jnp.clip(jax.random.normal(key_base, shape, jnp.float32), -6.0, 6.0)
    return (base * zscale[:, None, None] * chan[None, :, None]).astype(jnp.bfloat16)


def draw_x_field(key, part):
    key = jax.random.fold_in(key, 11)
    return scaled_field(key, CIN)


def draw_grad_out(key, part):
    key = jax.random.fold_in(key, 12)
    return scaled_field(key, COUT)


def block_scale(own_key, shape, shards, low, largest):
    gain, own = 1.0, jax.random.fold_in(own_key, 6)
    for axis_at, blocks in shards:
        steps = jnp.exp(jax.random.uniform(jax.random.fold_in(own, axis_at), (blocks,), jnp.float32, low / len(shards), largest / len(shards)))
        gain = gain * jnp.repeat(steps, shape[axis_at] // blocks).reshape([-1 if axis == axis_at else 1 for axis in range(len(shape))])
    return gain


def normal_values(stream_key, dims, spread, most, cuts=(), kind=jnp.bfloat16):
    loudness = block_scale(stream_key, dims, cuts, -0.22, 0.18) if cuts else 1.0
    drawn = jax.random.normal(stream_key, dims, jnp.float32) * spread * loudness
    return jnp.minimum(jnp.maximum(drawn, -most), most).astype(kind)


def setup_inputs(seed: int = 0) -> dict:
    arg_keys = jax.random.split(jax.random.key(seed), 4)
    x_field = draw_x_field(jax.random.fold_in(arg_keys[3], 71), 0)
    weights = normal_values(arg_keys[1], (COUT, KDIM), KDIM ** -0.5, 0.109375, ((0, 4),))
    grad_out = draw_grad_out(jax.random.fold_in(arg_keys[3], 71), 0)
    return dict(x_field=x_field, weights=weights, grad_out=grad_out)


def build_patches(window, planes, side):
    pieces = []
    for a in range(3):
        for b in range(3):
            for e in range(3):
                pieces.append(window[a:a + planes, b:b + side, e:e + side, :])
    stacked = jnp.stack(pieces, axis=-1)
    return stacked.reshape(planes * side * side, -1)

def reference(x_field, weights, grad_out):
    total = NZ * S * S
    x_last = jnp.transpose(x_field.astype(jnp.float32).reshape(NZ, CIN, S, S), (0, 2, 3, 1))
    x_pad = jnp.pad(x_last, ((1, 1), (1, 1), (1, 1), (0, 0)))
    w_full = weights.astype(jnp.float32).T
    grads = jnp.transpose(grad_out.astype(jnp.float32).reshape(NZ, COUT, S, S), (0, 2, 3, 1))
    hi = lax.Precision.HIGHEST

    def plane(carry, index):
        factor, wgrad = carry
        window = lax.dynamic_slice(x_pad, (index, jnp.int32(0), jnp.int32(0), jnp.int32(0)), (3, S + 2, S + 2, CIN))
        patches = build_patches(window, 1, S)
        out_plane = jnp.dot(patches, w_full, precision=hi).astype(jnp.bfloat16)
        dy_plane = lax.dynamic_slice(grads, (index, jnp.int32(0), jnp.int32(0), jnp.int32(0)), (1, S, S, COUT)).reshape(S * S, COUT)
        factor = factor + jnp.dot(patches.T, patches, precision=hi) / total
        wgrad = wgrad + jnp.dot(patches.T, dy_plane, precision=hi) / math.sqrt(total)
        return ((factor, wgrad), out_plane.T)
    start = (jnp.zeros((KDIM, KDIM), jnp.float32), jnp.zeros((KDIM, COUT), jnp.float32))
    (patch_factor, grad_weights), y_field = lax.scan(plane, start, jnp.arange(NZ, dtype=jnp.int32))
    dy_pad = jnp.pad(grads, ((1, 1), (1, 1), (1, 1), (0, 0)))
    w_taps = w_full.reshape(CIN, TAPS, COUT)
    acc = jnp.zeros((NZ * S * S, CIN), jnp.float32)
    for a in range(3):
        for b in range(3):
            for e in range(3):
                tap = 9 * a + 3 * b + e
                part = dy_pad[2 - a:2 - a + NZ, 2 - b:2 - b + S, 2 - e:2 - e + S, :].reshape(NZ * S * S, COUT)
                acc = acc + jnp.dot(part, w_taps[:, tap, :].T, precision=hi)
    grad_input = jnp.transpose(acc.reshape(NZ, S * S, CIN), (0, 2, 1)).astype(jnp.bfloat16)
    flat = grads.reshape(NZ * S * S, COUT)
    grad_factor = jnp.dot(flat.T, flat, precision=hi) / total
    return (y_field, grad_input, grad_weights, patch_factor, grad_factor)
```

```python
import jax
import jax.numpy as jnp
import numpy as np
from jax import lax
from jax.experimental import pallas as pl
from jax.experimental.pallas import tpu as pltpu
from jax.sharding import PartitionSpec as P

MESH = pl.DeviceIdType.MESH
BF, F32 = jnp.bfloat16, jnp.float32
SIDE, YX, TAPS = 32, 1024, 27
NT = (((1,), (1,)), ((), ()))


def kind(first, second):
    if first != second:
        return second - first + 2
    return {1: 2, 2: 5, 0: 6}[first]


def channel_order():
    out = np.zeros((128, 128), np.float32)
    for zi in range(8):
        for k in range(8):
            for p in range(2):
                out[zi * 16 + 2 * k + p, 16 * k + 2 * zi + p] = 1
    return out


def type_choice():
    out = np.zeros((144, 49), np.float32)
    for b2 in range(3):
        for e2 in range(3):
            for b in range(3):
                for e in range(3):
                    out[(b2 * 3 + e2) * 16 + b * 3 + e, kind(b, b2) * 7 + kind(e, e2)] = 1
    return out


def column_order():
    out = np.zeros((1152, 864), np.float32)
    for be in range(9):
        for a in range(3):
            for c in range(32):
                out[be * 128 + a * 32 + c, c * 27 + a * 9 + be] = 1
    return out


def moved(value, step):
    step = step % YX
    return value if step == 0 else pltpu.roll(value, shift=(YX - step) % YX, axis=1)


def cell_masks():
    cell = lax.broadcasted_iota(jnp.int32, (1, YX), 1)
    return cell // SIDE, cell % SIDE


def keep(where):
    return where.astype(F32).astype(BF)


def kernel(x_ref, g_ref, wy_ref, wg_ref, order_ref, choice_ref, column_ref,
           y_ref, gi_ref, gw_ref, pf_ref, gf_ref,
           xc, gc, gh, sp, rp, xr, xp, gp, rv, da, db, mg, rg, b3, rb, mp, rpf, gi, rgi, up, lh,
           send_sem, late_sem, xc_sem, gc_sem, gh_sem, sp_sem, rp_sem, rg_sem, rb_sem, rpf_sem, gi_sem):
    gz, col = lax.axis_index("gz"), lax.axis_index("col")
    k, z = gz // 8, gz % 8
    core = col + 1 - 2 * (col % 2)
    far = (col + 2) % 4
    diag = (core + 2) % 4
    above, below = (gz + 1) % 64, (gz + 63) % 64
    ring = [(z + j) % 8 for j in range(1, 8)]
    peers = [(k + j) % 8 for j in range(1, 8)]
    skip = jnp.where(z == 6, (gz + 3) % 64, (gz + 61) % 64)
    has_skip = jnp.logical_or(z == 1, z == 6)

    sends = []

    def send(src, dst, sem, target):
        copy = pltpu.make_async_remote_copy(
            src_ref=src, dst_ref=dst, send_sem=send_sem.at[len(sends)], recv_sem=sem,
            device_id=target, device_id_type=MESH)
        copy.start()
        sends.append(copy)

    def arrived(dst, sem):
        pltpu.make_async_remote_copy(
            src_ref=dst, dst_ref=dst, send_sem=send_sem.at[0], recv_sem=sem,
            device_id=(gz, core), device_id_type=MESH).wait_recv()

    barrier = pltpu.get_barrier_semaphore()
    partners = [(gz, core), (gz, far), (above, col), (below, col)]
    partners += [(k * 8 + zj, col) for zj in ring] + [(kj * 8 + z, col) for kj in peers]
    for target in partners:
        pl.semaphore_signal(barrier, inc=1, device_id=target, device_id_type=MESH)

    @pl.when(has_skip)
    def _():
        pl.semaphore_signal(barrier, inc=1, device_id=(skip, col), device_id_type=MESH)

    pl.semaphore_wait(barrier, len(partners) + jnp.where(has_skip, 1, 0))

    send(x_ref, xc.at[col, 1], xc_sem.at[col, 1], (gz, far))
    send(x_ref, xc.at[col, 1], xc_sem.at[col, 1], (gz, core))
    send(g_ref, gh.at[0], gh_sem.at[0], (above, col))
    send(g_ref, gh.at[1], gh_sem.at[1], (below, col))
    send(x_ref, xc.at[col, 0], xc_sem.at[col, 0], (above, col))
    send(x_ref, xc.at[col, 2], xc_sem.at[col, 2], (below, col))
    skip_out = jnp.where(z == 6, 0, 11)
    skip_in = jnp.where(z == 6, 11, 0)

    def skip_copy():
        return pltpu.make_async_remote_copy(
            src_ref=x_ref, dst_ref=sp.at[skip_out], send_sem=late_sem.at[0], recv_sem=sp_sem.at[skip_out],
            device_id=(skip, col), device_id_type=MESH)

    @pl.when(has_skip)
    def _():
        skip_copy().start()

    send(g_ref, gc.at[col], gc_sem.at[col], (gz, far))
    send(g_ref, gc.at[col], gc_sem.at[col], (gz, core))
    for zj in ring:
        send(x_ref, sp.at[2 + z], sp_sem.at[2 + z], (k * 8 + zj, col))
    xc[col, 1] = x_ref[...]
    gc[col] = g_ref[...]
    sp[2 + z] = x_ref[...]

    arrived(xc.at[far, 1], xc_sem.at[far, 1])
    send(xc.at[far, 1], xc.at[far, 1], xc_sem.at[far, 1], (gz, core))
    arrived(xc.at[core, 1], xc_sem.at[core, 1])
    arrived(xc.at[diag, 1], xc_sem.at[diag, 1])
    x_all = xc[:, 1].reshape(128, YX)
    xr[...] = jnp.dot(order_ref[...], x_all, preferred_element_type=F32).astype(BF).reshape(8, 16, YX)
    for zj in ring:
        send(xr.at[zj], rp.at[z], rp_sem.at[z], (k * 8 + zj, col))
    rp[z] = xr[z]

    for side, edge in ((0, 0), (2, 63)):
        arrived(xc.at[col, side], xc_sem.at[col, side])

        @pl.when(gz == edge)
        def _():
            xc[col, side] = jnp.zeros((32, YX), BF)

        send(xc.at[col, side], xc.at[col, side], xc_sem.at[col, side], (gz, far))
        send(xc.at[col, side], xc.at[col, side], xc_sem.at[col, side], (gz, core))

    @pl.when(has_skip)
    def _():
        arrived(sp.at[skip_in], sp_sem.at[skip_in])

    @pl.when(jnp.logical_and(z == 1, k == 0))
    def _():
        sp[0] = jnp.zeros((32, YX), BF)

    @pl.when(jnp.logical_and(z == 6, k == 7))
    def _():
        sp[11] = jnp.zeros((32, YX), BF)

    forwards = ((1, 0, lambda: sp.at[0]), (0, 1, lambda: xc.at[col, 0]),
                (7, 10, lambda: xc.at[col, 2]), (6, 11, lambda: sp.at[11]))

    def forward_copies(owner, slot, source):
        return [pltpu.make_async_remote_copy(
            src_ref=source(), dst_ref=sp.at[slot], send_sem=late_sem.at[1 + j], recv_sem=sp_sem.at[slot],
            device_id=(k * 8 + (owner + 1 + j) % 8, col), device_id_type=MESH) for j in range(7)]

    for owner, slot, source in forwards:
        @pl.when(z == owner)
        def _():
            for copy in forward_copies(owner, slot, source):
                copy.start()

    @pl.when(z == 0)
    def _():
        sp[1] = xc[col, 0]

    @pl.when(z == 7)
    def _():
        sp[10] = xc[col, 2]

    arrived(gc.at[far], gc_sem.at[far])
    send(gc.at[far], gc.at[far], gc_sem.at[far], (gz, core))

    row, place = cell_masks()
    in_row = {-1: keep(place >= 1), 1: keep(place < SIDE - 1)}
    in_plane = {-1: keep(row >= 1), 1: keep(row < SIDE - 1)}

    def shifted(value, dy, dx):
        if dx:
            value = moved(value, dx) * in_row[dx]
        if dy:
            value = moved(value, SIDE * dy) * in_plane[dy]
        return value

    for slot, edge in ((0, 0), (1, 63)):
        arrived(gh.at[slot], gh_sem.at[slot])

        @pl.when(gz == edge)
        def _():
            gh[slot] = jnp.zeros((64, YX), BF)

    for a in range(3):
        plane = (gh[1], g_ref[...], gh[0])[a]
        for e in range(3):
            line = shifted(plane, 0, 1 - e)
            for b in range(3):
                tap = 9 * a + 3 * b + e
                gp[tap * 64:(tap + 1) * 64, :] = shifted(line, 1 - b, 0)

    x_all = xc[:, 1].reshape(128, YX)
    grad_w = lax.dot_general(x_all, gp[...], NT, preferred_element_type=F32)
    for kj in range(8):
        mg[kj, :, 0:1728] = grad_w[16 * kj:16 * kj + 16]
        mg[kj, :, 1728:1792] = jnp.zeros((16, 64), F32)
    arrived(gc.at[core], gc_sem.at[core])
    arrived(gc.at[diag], gc_sem.at[diag])
    gram = lax.dot_general(gc[...].reshape(256, YX), g_ref[...], NT, preferred_element_type=F32)
    for kj in range(8):
        mg[kj, :, 1792:1856] = gram[32 * kj:32 * kj + 16]
        mg[kj, :, 1856:1920] = gram[32 * kj + 16:32 * kj + 32]
    for kj in peers:
        send(mg.at[kj], rg.at[k], rg_sem.at[k], (kj * 8 + z, col))

    gi[...] = jnp.dot(wg_ref[...], gp[...], preferred_element_type=F32).reshape(4, 32, YX)
    send(gi.at[core], rgi.at[0], gi_sem.at[0], (gz, core))
    send(gi.at[diag], rgi.at[1], gi_sem.at[1], (gz, core))

    for side in (0, 2):
        arrived(xc.at[far, side], xc_sem.at[far, side])
        send(xc.at[far, side], xc.at[far, side], xc_sem.at[far, side], (gz, core))
    arrived(rgi.at[1], gi_sem.at[1])
    up[...] = gi[far] + rgi[1]
    send(up, rgi.at[2], gi_sem.at[2], (gz, far))
    for side in (0, 2):
        arrived(xc.at[core, side], xc_sem.at[core, side])
        arrived(xc.at[diag, side], xc_sem.at[diag, side])

    for a in range(3):
        plane = xc[:, a].reshape(128, YX)
        for e in range(3):
            line = shifted(plane, 0, e - 1)
            for b in range(3):
                tap = 9 * a + 3 * b + e
                xp[tap * 128:(tap + 1) * 128, :] = shifted(line, b - 1, 0)
    y_ref[0] = jnp.dot(wy_ref[...], xp[...], preferred_element_type=F32).astype(BF)

    for zj in ring:
        arrived(rp.at[zj], rp_sem.at[zj])
        arrived(sp.at[2 + zj], sp_sem.at[2 + zj])
    for owner, slot, source in forwards:
        @pl.when(z != owner)
        def _():
            arrived(sp.at[slot], sp_sem.at[slot])

    da[...] = jnp.zeros((784, 128), F32)
    db[...] = jnp.zeros((784, 128), F32)
    edge_plane = jnp.where(k < 4, 0, 7)

    def variants(value, unit, at, size):
        out = []
        for delta in (-2, -1, 0, 1, 2):
            inside = jnp.logical_and(at - delta >= 0, at - delta < size)
            out.append(value if delta == 0 else moved(value, -delta * unit) * keep(inside))
        out.append(value * keep(at >= 1))
        out.append(value * keep(at < size - 1))
        return out

    @pl.loop(0, 8)
    def _(v):
        rows = rp[v]
        for tx, line in enumerate(variants(rows, 1, place, SIDE)):
            for ty, plane in enumerate(variants(line, SIDE, row, SIDE)):
                at = (ty * 7 + tx) * 16
                rv[at:at + 16, :] = plane
        near = sp[pl.ds(v, 5)].reshape(160, YX)
        flag = jnp.where(v == edge_plane, 1.0, 0.0).astype(BF)
        columns = jnp.concatenate([near, sp[v + 2] * flag], axis=0)
        part = lax.dot_general(rv[...], columns, NT, preferred_element_type=F32)
        da[...] += part[:, 0:128]
        db[:, 0:64] += part[:, 128:192]

    lane = lax.broadcasted_iota(jnp.int32, (49, 128), 1)
    for kj in range(8):
        tails = []
        for p in range(2):
            mp[kj, p] = da[pl.ds(2 * kj + p, 49, stride=16), :]
            tails.append(db[pl.ds(2 * kj + p, 49, stride=16), :])
        mp[kj, 2] = jnp.where(lane < 64, tails[0], pltpu.roll(tails[1], shift=64, axis=1))
    for kj in peers:
        send(mp.at[kj], rpf.at[k], rpf_sem.at[k], (kj * 8 + z, col))

    total = mg[k]
    for kj in peers:
        arrived(rg.at[kj], rg_sem.at[kj])
        total = total + rg[kj]
    for j in range(14):
        for zj in range(8):
            b3[zj, 2 * j:2 * j + 2, :] = total[2 * zj:2 * zj + 2, 128 * j:128 * j + 128]
    halves = (total[:, 1792:1920], pltpu.roll(total[:, 1792:1920], shift=64, axis=1))
    for zj in range(8):
        b3[zj, 28:32, :] = halves[zj // 4][4 * (zj % 4):4 * (zj % 4) + 4]
    for zj in ring:
        send(b3.at[zj], rb.at[z], rb_sem.at[z], (k * 8 + zj, col))

    arrived(rgi.at[0], gi_sem.at[0])
    arrived(rgi.at[2], gi_sem.at[2])
    gi_ref[0] = (gi[col] + rgi[0] + rgi[2]).astype(BF)

    for kj in peers:
        arrived(rpf.at[kj], rpf_sem.at[kj])
    rpf[k] = mp[k]
    heads = [rpf[0, p] for p in range(2)]
    tail = rpf[0, 2]
    low, high = rpf[0, 2], rpf[7, 2]
    for kj in range(1, 8):
        heads = [heads[p] + rpf[kj, p] for p in range(2)]
        tail = tail + rpf[kj, 2]
    pad = jnp.zeros((49, 32), F32)
    for p in range(2):
        m2, m1, zero, p1 = [heads[p][:, 32 * i:32 * i + 32] for i in range(4)]
        p2 = tail[:, 64 * p:64 * p + 32]
        first = low[:, 64 * p + 32:64 * p + 64]
        last = high[:, 64 * p + 32:64 * p + 64]
        wide = jnp.concatenate(
            [zero - last, p1, p2, pad, m1, zero, p1, pad, m2, m1, zero - first, pad], axis=1)
        for part in range(3):
            piece = wide.astype(BF)
            wide = wide - piece.astype(F32)
            picked = jnp.dot(choice_ref[...], piece, preferred_element_type=F32).astype(BF)
            for a in range(3):
                at = (part * 6 + p * 3 + a) * 16
                for be in range(9):
                    lh[at:at + 16, be * 128:be * 128 + 128] = picked[be * 16:be * 16 + 16, a * 128:a * 128 + 128]
    factor = jnp.dot(lh[...], column_ref[...], preferred_element_type=F32)
    factor = (factor[0:96] + factor[96:192] + factor[192:288]) * (1.0 / 65536)
    for block in range(6):
        pf_ref[block * 9:block * 9 + 9, :] = factor[block * 16:block * 16 + 9]

    total = b3[z]
    for zj in ring:
        arrived(rb.at[zj], rb_sem.at[zj])
        total = total + rb[zj]
    gf_ref[...] = total[28:32, 0:64] * (1.0 / 65536)
    for tap in range(TAPS):
        for p in range(2):
            at = 2 * (tap // 2) + p
            gw_ref[p * 27 + tap:p * 27 + tap + 1, :] = total[at:at + 1, 64 * (tap % 2):64 * (tap % 2) + 64] * (1.0 / 256)

    for copy in sends:
        copy.wait_send()

    @pl.when(has_skip)
    def _():
        skip_copy().wait_send()

    for owner, slot, source in forwards:
        @pl.when(z == owner)
        def _():
            for copy in forward_copies(owner, slot, source):
                copy.wait_send()


def shards(x_field, weights, grad_out):
    taps = weights.reshape(64, 128, TAPS)
    wy = jnp.transpose(taps, (0, 2, 1)).reshape(64, TAPS * 128)
    wg = jnp.transpose(taps, (1, 2, 0)).reshape(128, TAPS * 64)
    vmem = pl.BlockSpec(memory_space=pltpu.VMEM)
    dma = pltpu.SemaphoreType.DMA
    return pl.pallas_call(
        kernel,
        out_shape=(
            jax.ShapeDtypeStruct((1, 64, YX), BF),
            jax.ShapeDtypeStruct((1, 32, YX), BF),
            jax.ShapeDtypeStruct((54, 64), F32),
            jax.ShapeDtypeStruct((54, 864), F32),
            jax.ShapeDtypeStruct((4, 64), F32),
        ),
        in_specs=[vmem] * 7,
        out_specs=(vmem,) * 5,
        scratch_shapes=[
            pltpu.VMEM((4, 3, 32, YX), BF),
            pltpu.VMEM((4, 64, YX), BF),
            pltpu.VMEM((2, 64, YX), BF),
            pltpu.VMEM((12, 32, YX), BF),
            pltpu.VMEM((8, 16, YX), BF),
            pltpu.VMEM((8, 16, YX), BF),
            pltpu.VMEM((3456, YX), BF),
            pltpu.VMEM((1728, YX), BF),
            pltpu.VMEM((784, YX), BF),
            pltpu.VMEM((784, 128), F32),
            pltpu.VMEM((784, 128), F32),
            pltpu.VMEM((8, 16, 1920), F32),
            pltpu.VMEM((8, 16, 1920), F32),
            pltpu.VMEM((8, 32, 128), F32),
            pltpu.VMEM((8, 32, 128), F32),
            pltpu.VMEM((8, 3, 49, 128), F32),
            pltpu.VMEM((8, 3, 49, 128), F32),
            pltpu.VMEM((4, 32, YX), F32),
            pltpu.VMEM((3, 32, YX), F32),
            pltpu.VMEM((32, YX), F32),
            pltpu.VMEM((288, 1152), BF),
            dma((64,)),
            dma((8,)),
            dma((4, 3)),
            dma((4,)),
            dma((2,)),
            dma((12,)),
            dma((8,)),
            dma((8,)),
            dma((8,)),
            dma((8,)),
            dma((3,)),
        ],
        compiler_params=pltpu.CompilerParams(
            collective_id=0, has_side_effects=True, vmem_limit_bytes=48 * 2**20),
    )(x_field.reshape(32, YX), grad_out.reshape(64, YX), wy, wg,
      jnp.asarray(channel_order(), BF), jnp.asarray(type_choice(), BF), jnp.asarray(column_order(), BF))


def solution(mesh):
    return jax.shard_map(
        shards,
        mesh=mesh,
        in_specs=(P("gz", "col", None), P("col", None), P("gz", "col", None)),
        out_specs=(
            P("gz", "col", None),
            P("gz", "col", None),
            P("gz", "col"),
            P("gz", "col"),
            P("gz", "col"),
        ),
        check_vma=False,
    )
```

```python
import jax
import jax.numpy as jnp
import numpy as np
from jax import lax
from jax.experimental import pallas as pl
from jax.experimental.pallas import tpu as pltpu
from jax.sharding import PartitionSpec as P

MESH = pl.DeviceIdType.MESH
BF, F32 = jnp.bfloat16, jnp.float32
SIDE, YX, TAPS = 32, 1024, 27
NT = (((1,), (1,)), ((), ()))


def kind(first, second):
    if first != second:
        return second - first + 2
    return {1: 2, 2: 5, 0: 6}[first]


def channel_order():
    out = np.zeros((128, 128), np.float32)
    for v in range(8):
        for k in range(8):
            for p in range(2):
                out[v * 16 + 2 * k + p, k // 2 * 32 + v * 4 + 2 * (k % 2) + p] = 1
    return out


def type_choice():
    out = np.zeros((144, 49), np.float32)
    for b2 in range(3):
        for e2 in range(3):
            for b in range(3):
                for e in range(3):
                    out[(b2 * 3 + e2) * 16 + b * 3 + e, kind(b, b2) * 7 + kind(e, e2)] = 1
    return out


def moved(value, step):
    step = step % YX
    return value if step == 0 else pltpu.roll(value, shift=(YX - step) % YX, axis=1)


def cell_masks():
    cell = lax.broadcasted_iota(jnp.int32, (1, YX), 1)
    return cell // SIDE, cell % SIDE


def keep(where):
    return where.astype(F32).astype(BF)


def kernel(x_hbm, g_hbm, w_hbm, order_hbm, choice_hbm,
           y_ref, gi_ref, gw_ref, pf_ref, gf_ref,
           g_ref, w_ref, order_ref, choice_ref, column_ref, wt, wy, wg,
           xc, gc, gs, sp, r4, rp, r9, xp, gp, rv, da, db, ga, gb, mg, rg, b3, rb, mp, rpf, mw, rw, me, re, gi, rgi, up, lh,
           send_sem, late_sem, load_sem, xc_sem, gc_sem, gs_sem, sp_sem, r4_sem, rg_sem, rb_sem, rpf_sem, rw_sem, re_sem,
           gi_sem):
    gz, col = lax.axis_index("gz"), lax.axis_index("col")
    k, z = gz // 8, gz % 8
    core = col + 1 - 2 * (col % 2)
    far = (col + 2) % 4
    diag = (core + 2) % 4
    ring = [(z + j) % 8 for j in (1, 7, 2, 6, 3, 5, 4)]
    peers = [(k + j) % 8 for j in range(1, 8)]
    x_own, g_own = x_hbm.at[0], g_hbm.at[0]

    def on_ring(offset):
        return (k * 8 + (z + offset) % 8, col)

    sends = []

    def send(src, dst, sem, target):
        copy = pltpu.make_async_remote_copy(
            src_ref=src, dst_ref=dst, send_sem=send_sem.at[len(sends)], recv_sem=sem,
            device_id=target, device_id_type=MESH)
        copy.start()
        sends.append(copy)

    def arrived(dst, sem):
        pltpu.make_async_remote_copy(
            src_ref=dst, dst_ref=dst, send_sem=send_sem.at[0], recv_sem=sem,
            device_id=(gz, core), device_id_type=MESH).wait_recv()

    loads = [pltpu.make_async_copy(src, dst, load_sem.at[i]) for i, (src, dst) in enumerate((
        (w_hbm, w_ref), (g_own, g_ref), (x_own, xc.at[col, 1]), (x_own, sp.at[2 + z]), (g_own, gc.at[col]), (g_own, gs.at[1 + z]),
        (order_hbm, order_ref), (choice_hbm, choice_ref)))]
    for load in loads:
        load.start()

    barrier = pltpu.get_barrier_semaphore()
    partners = [(gz, core), (gz, far)]
    partners += [(k * 8 + zj, col) for zj in ring] + [(kj * 8 + z, col) for kj in peers]
    for target in partners:
        pl.semaphore_signal(barrier, inc=1, device_id=target, device_id_type=MESH)
    loads[0].wait()
    wt[:, 0:64] = jnp.transpose(w_ref[...].astype(F32))
    wt[:, 64:128] = jnp.zeros((3456, 64), F32)
    for tap in range(TAPS):
        block = wt[pl.ds(tap, 128, stride=TAPS), :]
        wg[:, tap * 64:tap * 64 + 64] = block[:, 0:64].astype(BF)
        wy[:, tap * 128:tap * 128 + 128] = jnp.transpose(block)[0:64].astype(BF)
    entry = lax.broadcasted_iota(jnp.int32, (128, 864), 0)
    column = lax.broadcasted_iota(jnp.int32, (128, 864), 1)
    home = jnp.where(entry < 96, entry % 32 * 27 + entry // 32 * 9, -27)
    for be in range(9):
        column_ref[be * 128:be * 128 + 128, :] = keep(column == home + be)
    for load in loads[1:]:
        load.wait()

    row, place = cell_masks()
    in_row = {-1: keep(place >= 1), 1: keep(place < SIDE - 1)}
    in_plane = {-1: keep(row >= 1), 1: keep(row < SIDE - 1)}

    def shifted(value, dy, dx):
        if dx:
            value = moved(value, dx) * in_row[dx]
        if dy:
            value = moved(value, SIDE * dy) * in_plane[dy]
        return value

    def cotangent_taps(a, plane):
        for e in range(3):
            line = shifted(plane, 0, 1 - e)
            for b in range(3):
                tap = 9 * a + 3 * b + e
                gp[tap * 64:(tap + 1) * 64, :] = shifted(line, 1 - b, 0)

    cotangent_taps(1, g_ref[...])
    pl.semaphore_wait(barrier, len(partners))

    def edge_copies(buf, sem, base, edges):
        return [(plane, pltpu.make_async_remote_copy(
            src_ref=buf.at[base + plane], dst_ref=buf.at[home], send_sem=late_sem.at[late], recv_sem=sem.at[home],
            device_id=((k + step) % 8 * 8 + z, col), device_id_type=MESH)) for plane, home, step, late in edges]

    x_edges = edge_copies(sp, sp_sem, 2, ((0, 10, 7, 0), (1, 11, 7, 1), (6, 0, 1, 2), (7, 1, 1, 3)))
    g_edges = edge_copies(gs, gs_sem, 1, ((0, 9, 7, 4), (7, 0, 1, 5)))

    def pass_on(buf, sem, base, edges, offset, steps):
        at = (z + offset) % 8
        slot = base + at
        if offset:
            arrived(buf.at[slot], sem.at[slot])
        for step in steps:
            send(buf.at[slot], buf.at[slot], sem.at[slot], on_ring(step))
        for plane, copy in edges:
            @pl.when(at == plane)
            def _():
                copy.start()

    def pass_x(offset, *steps):
        pass_on(sp, sp_sem, 2, x_edges, offset, steps)

    def pass_g(offset, *steps):
        pass_on(gs, gs_sem, 1, g_edges, offset, steps)

    def others(buf, sem):
        send(buf, buf, sem, (gz, far))
        send(buf, buf, sem, (gz, core))

    def hand_over(buf, sem):
        arrived(buf, sem)
        send(buf, buf, sem, (gz, core))

    pass_x(0, 1, 7)
    others(xc.at[col, 1], xc_sem.at[col, 1])
    pass_g(0, 1, 7)
    pass_x(7, 1)
    pass_x(1, 7)
    hand_over(xc.at[far, 1], xc_sem.at[far, 1])
    pass_x(6, 1)
    pass_x(2, 7)
    pass_g(7, 1)
    pass_g(1, 7)
    pass_x(5, 1)
    pass_x(3)
    pass_x(4)

    pick = lax.broadcasted_iota(jnp.int32, (32, 256), 0)
    source = lax.broadcasted_iota(jnp.int32, (32, 256), 1)
    wanted = pick // 4 * 32 + pick // 2 % 2 * 16 + 2 * z + pick % 2
    r4[col] = jnp.dot(keep(source == wanted), sp[2:10].reshape(256, YX), preferred_element_type=F32).astype(BF)
    others(r4.at[col], r4_sem.at[col])
    others(gc.at[col], gc_sem.at[col])
    pass_g(6, 1)
    pass_g(2, 7)
    hand_over(r4.at[far], r4_sem.at[far])
    arrived(r4.at[core], r4_sem.at[core])
    arrived(r4.at[diag], r4_sem.at[diag])
    rp[...] = jnp.dot(
        order_ref[...], r4[...].reshape(128, YX), preferred_element_type=F32).astype(BF).reshape(8, 16, YX)

    da[...] = jnp.zeros((784, 128), F32)
    db[...] = jnp.zeros((800, 128), F32)
    edge_plane = jnp.where(k < 4, 0, 7)

    def variants(value, unit, at, size):
        out = []
        for delta in (-2, -1, 0, 1, 2):
            inside = jnp.logical_and(at - delta >= 0, at - delta < size)
            out.append(value if delta == 0 else moved(value, -delta * unit) * keep(inside))
        out.append(value * keep(at >= 1))
        out.append(value * keep(at < size - 1))
        return out

    def factor_plane(v):
        rows = rp[v]
        for tx, line in enumerate(variants(rows, 1, place, SIDE)):
            for ty, plane in enumerate(variants(line, SIDE, row, SIDE)):
                at = (ty * 7 + tx) * 16
                rv[at:at + 16, :] = plane
        for b in range(3):
            for e in range(3):
                at = ((3 - b) * 7 + 3 - e) * 16
                r9[v, (3 * b + e) * 16:(3 * b + e) * 16 + 16, :] = rv[at:at + 16, :]
        beside = sp[pl.ds(v, 5)].reshape(160, YX)
        flag = jnp.where(v == edge_plane, 1.0, 0.0).astype(BF)
        columns = jnp.concatenate([beside, sp[v + 2] * flag], axis=0)
        part = lax.dot_general(rv[...], columns, NT, preferred_element_type=F32)
        da[...] += part[:, 0:128]
        db[0:784, 0:64] += part[:, 128:192]

    @pl.loop(2, 4)
    def _(v):
        factor_plane(v)

    pass_g(5, 1)
    pass_g(3)

    @pl.loop(4, 6)
    def _(v):
        factor_plane(v)

    pass_g(4)
    hand_over(gc.at[far], gc_sem.at[far])
    for buf, sem, slot, edge in ((sp, sp_sem, 0, 0), (sp, sp_sem, 1, 0), (sp, sp_sem, 10, 7), (sp, sp_sem, 11, 7)):
        arrived(buf.at[slot], sem.at[slot])

        @pl.when(k == edge)
        def _():
            buf[slot] = jnp.zeros(buf.shape[1:], BF)

    for side in (0, 2):
        xc[col, side] = sp[1 + z + side]
        others(xc.at[col, side], xc_sem.at[col, side])

    @pl.loop(6, 10)
    def _(v):
        factor_plane(v % 8)

    lane = lax.broadcasted_iota(jnp.int32, (25, 128), 1)

    def packed(kj, first):
        out = None
        for q in range(4):
            run = db[pl.ds(2 * kj + q // 2 + 400 * (q % 2), 25, stride=16), :]
            step = (32 * q - first) % 128
            run = pltpu.roll(run, shift=step, axis=1) if step else run
            out = run if out is None else jnp.where(lane // 32 == q, run, out)
        return out

    for kj in range(8):
        for p in range(2):
            mp[kj, 49 * p:49 * p + 49] = da[pl.ds(2 * kj + p, 49, stride=16), :]
        mp[kj, 98:123] = packed(kj, 0)
    for kj in peers:
        send(mp.at[kj], rpf.at[k], rpf_sem.at[k], (kj * 8 + z, col))
    def face_copies(owner):
        return [pltpu.make_async_remote_copy(
            src_ref=me.at[(owner + j) % 8], dst_ref=re.at[owner // 7], send_sem=late_sem.at[24 + j],
            recv_sem=re_sem.at[owner // 7], device_id=((owner + j) % 8 * 8 + z, col),
            device_id_type=MESH) for j in range(1, 8)]

    for owner in (0, 7):
        @pl.when(k == owner)
        def _():
            for kj in range(8):
                me[kj] = packed(kj, 32)
            for copy in face_copies(owner):
                copy.start()
            re[owner // 7] = me[owner]

    for slot, edge in ((0, 0), (9, 7)):
        arrived(gs.at[slot], gs_sem.at[slot])

        @pl.when(k == edge)
        def _():
            gs[slot] = jnp.zeros((64, YX), BF)

    cotangent_taps(0, gs[2 + z])
    cotangent_taps(2, gs[z])
    gi[...] = jnp.dot(wg[...], gp[...], preferred_element_type=F32).reshape(4, 32, YX)
    send(gi.at[core], rgi.at[0], gi_sem.at[0], (gz, core))
    send(gi.at[diag], rgi.at[1], gi_sem.at[1], (gz, core))

    ga[...] = jnp.zeros((144, 128), F32)
    gb[...] = jnp.zeros((144, 128), F32)

    @pl.loop(0, 8)
    def _(v):
        part = lax.dot_general(
            r9[v], gs[pl.ds(v, 3)].reshape(192, YX), NT, preferred_element_type=F32)
        ga[...] += part[:, 0:128]
        gb[:, 0:64] += part[:, 128:192]

    wide_lane = lax.broadcasted_iota(jnp.int32, (9, 128), 1)
    for kj in range(8):
        tails = []
        for p in range(2):
            mw[kj, 9 * p:9 * p + 9] = ga[pl.ds(2 * kj + p, 9, stride=16), :]
            tails.append(gb[pl.ds(2 * kj + p, 9, stride=16), :])
        mw[kj, 18:27] = jnp.where(wide_lane < 64, tails[0], pltpu.roll(tails[1], shift=64, axis=1))
    for kj in peers:
        send(mw.at[kj], rw.at[k], rw_sem.at[k], (kj * 8 + z, col))

    arrived(gc.at[core], gc_sem.at[core])
    arrived(gc.at[diag], gc_sem.at[diag])
    gram = lax.dot_general(gc[...].reshape(256, YX), g_ref[...], NT, preferred_element_type=F32)
    for kj in range(8):
        mg[kj, :, 0:64] = gram[32 * kj:32 * kj + 16]
        mg[kj, :, 64:128] = gram[32 * kj + 16:32 * kj + 32]
    for kj in peers:
        send(mg.at[kj], rg.at[k], rg_sem.at[k], (kj * 8 + z, col))

    arrived(rgi.at[1], gi_sem.at[1])
    up[...] = gi[far] + rgi[1]
    send(up, rgi.at[2], gi_sem.at[2], (gz, far))
    for side in (0, 2):
        hand_over(xc.at[far, side], xc_sem.at[far, side])

    arrived(xc.at[core, 1], xc_sem.at[core, 1])
    arrived(xc.at[diag, 1], xc_sem.at[diag, 1])
    for side in (0, 2):
        arrived(xc.at[core, side], xc_sem.at[core, side])
        arrived(xc.at[diag, side], xc_sem.at[diag, side])

    for a in range(3):
        plane = xc[:, a].reshape(128, YX)
        for e in range(3):
            line = shifted(plane, 0, e - 1)
            for b in range(3):
                tap = 9 * a + 3 * b + e
                xp[tap * 128:(tap + 1) * 128, :] = shifted(line, b - 1, 0)
    y_ref[0] = jnp.dot(wy[...], xp[...], preferred_element_type=F32).astype(BF)

    total = mg[k]
    for kj in peers:
        arrived(rg.at[kj], rg_sem.at[kj])
        total = total + rg[kj]
    halves = (total, pltpu.roll(total, shift=64, axis=1))
    for zj in range(8):
        b3[zj] = halves[zj // 4][4 * (zj % 4):4 * (zj % 4) + 4]
    for zj in ring:
        send(b3.at[zj], rb.at[z], rb_sem.at[z], (k * 8 + zj, col))

    arrived(rgi.at[0], gi_sem.at[0])
    arrived(rgi.at[2], gi_sem.at[2])
    gi_ref[0] = (gi[col] + rgi[0] + rgi[2]).astype(BF)

    total = mp[k]
    for kj in peers:
        arrived(rpf.at[kj], rpf_sem.at[kj])
        total = total + rpf[kj]
    for owner in (0, 7):
        @pl.when(k != owner)
        def _():
            arrived(re.at[owner // 7], re_sem.at[owner // 7])
    low, high = re[0], re[1]
    pad = jnp.zeros((49, 32), F32)

    def unpacked(value, p):
        at = 64 * p
        return jnp.concatenate([value[0:25, at:at + 32], value[0:24, at + 32:at + 64]], axis=0)

    for p in range(2):
        head = total[49 * p:49 * p + 49]
        m2, m1, zero, p1 = [head[:, 32 * i:32 * i + 32] for i in range(4)]
        p2 = unpacked(total[98:123], p)
        first, last = unpacked(low, p), unpacked(high, p)
        wide = jnp.concatenate(
            [zero - last, p1, p2, pad, m1, zero, p1, pad, m2, m1, zero - first, pad], axis=1)
        for part in range(3):
            piece = wide.astype(BF)
            wide = wide - piece.astype(F32)
            picked = jnp.dot(choice_ref[...], piece, preferred_element_type=F32).astype(BF)
            for a in range(3):
                at = (part * 6 + p * 3 + a) * 16
                for be in range(9):
                    lh[at:at + 16, be * 128:be * 128 + 128] = picked[be * 16:be * 16 + 16, a * 128:a * 128 + 128]
    factor = jnp.dot(lh[...], column_ref[...], preferred_element_type=F32)
    factor = (factor[0:96] + factor[96:192] + factor[192:288]) * (1.0 / 65536)
    for block in range(6):
        pf_ref[block * 9:block * 9 + 9, :] = factor[block * 16:block * 16 + 9]

    total = mw[k]
    for kj in peers:
        arrived(rw.at[kj], rw_sem.at[kj])
        total = total + rw[kj]
    total = total * (1.0 / 256)
    for p in range(2):
        gw_ref[p * 27:p * 27 + 9, :] = total[18:27, 64 * p:64 * p + 64]
        gw_ref[p * 27 + 9:p * 27 + 18, :] = total[9 * p:9 * p + 9, 64:128]
        gw_ref[p * 27 + 18:p * 27 + 27, :] = total[9 * p:9 * p + 9, 0:64]

    total = b3[z]
    for zj in ring:
        arrived(rb.at[zj], rb_sem.at[zj])
        total = total + rb[zj]
    gf_ref[...] = total[:, 0:64] * (1.0 / 65536)

    for _, copy in x_edges + g_edges:
        copy.wait_send()
    for copy in sends:
        copy.wait_send()
    for owner in (0, 7):
        @pl.when(k == owner)
        def _():
            for copy in face_copies(owner):
                copy.wait_send()


def shards(x_field, weights, grad_out):
    vmem = pl.BlockSpec(memory_space=pltpu.VMEM)
    there = pl.BlockSpec(memory_space=pl.ANY)
    dma = pltpu.SemaphoreType.DMA
    return pl.pallas_call(
        kernel,
        out_shape=(
            jax.ShapeDtypeStruct((1, 64, YX), BF),
            jax.ShapeDtypeStruct((1, 32, YX), BF),
            jax.ShapeDtypeStruct((54, 64), F32),
            jax.ShapeDtypeStruct((54, 864), F32),
            jax.ShapeDtypeStruct((4, 64), F32),
        ),
        in_specs=[there] * 5,
        out_specs=(vmem,) * 5,
        scratch_shapes=[
            pltpu.VMEM((64, YX), BF),
            pltpu.VMEM((64, 3456), BF),
            pltpu.VMEM((128, 128), BF),
            pltpu.VMEM((144, 49), BF),
            pltpu.VMEM((1152, 864), BF),
            pltpu.VMEM((3456, 128), F32),
            pltpu.VMEM((64, 3456), BF),
            pltpu.VMEM((128, 1728), BF),
            pltpu.VMEM((4, 3, 32, YX), BF),
            pltpu.VMEM((4, 64, YX), BF),
            pltpu.VMEM((10, 64, YX), BF),
            pltpu.VMEM((12, 32, YX), BF),
            pltpu.VMEM((4, 32, YX), BF),
            pltpu.VMEM((8, 16, YX), BF),
            pltpu.VMEM((8, 144, YX), BF),
            pltpu.VMEM((3456, YX), BF),
            pltpu.VMEM((1728, YX), BF),
            pltpu.VMEM((784, YX), BF),
            pltpu.VMEM((784, 128), F32),
            pltpu.VMEM((800, 128), F32),
            pltpu.VMEM((144, 128), F32),
            pltpu.VMEM((144, 128), F32),
            pltpu.VMEM((8, 16, 128), F32),
            pltpu.VMEM((8, 16, 128), F32),
            pltpu.VMEM((8, 4, 128), F32),
            pltpu.VMEM((8, 4, 128), F32),
            pltpu.VMEM((8, 123, 128), F32),
            pltpu.VMEM((8, 123, 128), F32),
            pltpu.VMEM((8, 27, 128), F32),
            pltpu.VMEM((8, 27, 128), F32),
            pltpu.VMEM((8, 25, 128), F32),
            pltpu.VMEM((2, 25, 128), F32),
            pltpu.VMEM((4, 32, YX), F32),
            pltpu.VMEM((3, 32, YX), F32),
            pltpu.VMEM((32, YX), F32),
            pltpu.VMEM((288, 1152), BF),
            dma((72,)),
            dma((32,)),
            dma((8,)),
            dma((4, 3)),
            dma((4,)),
            dma((10,)),
            dma((12,)),
            dma((4,)),
            dma((8,)),
            dma((8,)),
            dma((8,)),
            dma((8,)),
            dma((2,)),
            dma((3,)),
        ],
        compiler_params=pltpu.CompilerParams(
            collective_id=0, has_side_effects=True, vmem_limit_bytes=56 * 2**20),
    )(x_field, grad_out, weights,
      jnp.asarray(channel_order(), BF), jnp.asarray(type_choice(), BF))


def solution(mesh):
    return jax.shard_map(
        shards,
        mesh=mesh,
        in_specs=(P("gz", "col", None), P("col", None), P("gz", "col", None)),
        out_specs=(
            P("gz", "col", None),
            P("gz", "col", None),
            P("gz", "col"),
            P("gz", "col"),
            P("gz", "col"),
        ),
        check_vma=False,
    )
```

```python
import jax
import jax.numpy as jnp
import numpy as np
from jax import lax
from jax.experimental import pallas as pl
from jax.experimental.pallas import tpu as pltpu
from jax.sharding import PartitionSpec as P

MESH = pl.DeviceIdType.MESH
BF, F32 = jnp.bfloat16, jnp.float32
SIDE, YX, TAPS = 32, 1024, 27
NT = (((1,), (1,)), ((), ()))


def kind(first, second):
    if first != second:
        return second - first + 2
    return {1: 2, 2: 5, 0: 6}[first]


def channel_order():
    out = np.zeros((128, 128), np.float32)
    for v in range(8):
        for k in range(8):
            for p in range(2):
                out[v * 16 + 2 * k + p, k // 2 * 32 + v * 4 + 2 * (k % 2) + p] = 1
    return out


def type_choice():
    out = np.zeros((144, 49), np.float32)
    for b2 in range(3):
        for e2 in range(3):
            for b in range(3):
                for e in range(3):
                    out[(b2 * 3 + e2) * 16 + b * 3 + e, kind(b, b2) * 7 + kind(e, e2)] = 1
    return out


def moved(value, step):
    step = step % YX
    return value if step == 0 else pltpu.roll(value, shift=(YX - step) % YX, axis=1)


def cell_masks():
    cell = lax.broadcasted_iota(jnp.int32, (1, YX), 1)
    return cell // SIDE, cell % SIDE


def keep(where):
    return where.astype(F32).astype(BF)


def kernel(x_hbm, g_hbm, w_hbm, order_hbm, choice_hbm,
           y_ref, gi_ref, gw_ref, pf_ref, gf_ref,
           g_ref, w_ref, order_ref, choice_ref, column_ref, wt, wy, wg,
           xc, gc, gh, sp, r4, rp, xp, gp, rv, da, db, mg, rg, mx, rx, b3, rb, mp, rpf, me, re, gi, rgi, up, lh,
           send_sem, late_sem, load_sem, xc_sem, gc_sem, gh_sem, sp_sem, r4_sem, rg_sem, rx_sem, rb_sem, rpf_sem, re_sem,
           gi_sem):
    gz, col = lax.axis_index("gz"), lax.axis_index("col")
    k, z = gz // 8, gz % 8
    core = col + 1 - 2 * (col % 2)
    far = (col + 2) % 4
    diag = (core + 2) % 4
    ring = [(z + j) % 8 for j in (1, 7, 2, 6, 3, 5, 4)]
    peers = [(k + j) % 8 for j in range(1, 8)]
    x_own, g_own = x_hbm.at[0], g_hbm.at[0]

    def on_ring(offset):
        return (k * 8 + (z + offset) % 8, col)

    sends = []

    def send(src, dst, sem, target):
        copy = pltpu.make_async_remote_copy(
            src_ref=src, dst_ref=dst, send_sem=send_sem.at[len(sends)], recv_sem=sem,
            device_id=target, device_id_type=MESH)
        copy.start()
        sends.append(copy)

    def arrived(dst, sem):
        pltpu.make_async_remote_copy(
            src_ref=dst, dst_ref=dst, send_sem=send_sem.at[0], recv_sem=sem,
            device_id=(gz, core), device_id_type=MESH).wait_recv()

    barrier = pltpu.get_barrier_semaphore()
    above, below = (gz + 1) % 64, (gz + 63) % 64
    xl, yk = k // 4, k % 4
    partners = [(gz, core), (gz, far), (above, col), (below, col)]
    partners += [(k * 8 + zj, col) for zj in ring] + [(kj * 8 + z, col) for kj in peers]
    for target in partners:
        pl.semaphore_signal(barrier, inc=1, device_id=target, device_id_type=MESH)
    loads = [pltpu.make_async_copy(src, dst, load_sem.at[i]) for i, (src, dst) in enumerate((
        (w_hbm, w_ref), (g_own, g_ref), (x_own, xc.at[col, 1]), (x_own, sp.at[2 + z]), (g_own, gc.at[col]),
        (order_hbm, order_ref), (choice_hbm, choice_ref)))]
    for load in loads:
        load.start()
    row, place = cell_masks()
    in_row = {-1: keep(place >= 1), 1: keep(place < SIDE - 1)}
    in_plane = {-1: keep(row >= 1), 1: keep(row < SIDE - 1)}

    def shifted(value, dy, dx):
        if dx:
            value = moved(value, dx) * in_row[dx]
        if dy:
            value = moved(value, SIDE * dy) * in_plane[dy]
        return value

    def cotangent_taps(a, plane):
        for e in range(3):
            line = shifted(plane, 0, 1 - e)
            for b in range(3):
                tap = 9 * a + 3 * b + e
                gp[tap * 64:(tap + 1) * 64, :] = shifted(line, 1 - b, 0)

    x_loads, other_loads = loads[2:4], loads[1:2] + loads[4:]
    for load in x_loads:
        load.wait()
    pl.semaphore_wait(barrier, len(partners))

    def edge_copies(buf, sem, base, edges):
        return [(plane, pltpu.make_async_remote_copy(
            src_ref=buf.at[base + plane], dst_ref=buf.at[home], send_sem=late_sem.at[late], recv_sem=sem.at[home],
            device_id=((k + step) % 8 * 8 + z, col), device_id_type=MESH)) for plane, home, step, late in edges]

    x_edges = edge_copies(sp, sp_sem, 2, ((0, 10, 7, 0), (1, 11, 7, 1), (6, 0, 1, 2), (7, 1, 1, 3)))

    def pass_on(buf, sem, base, edges, offset, steps):
        at = (z + offset) % 8
        slot = base + at
        if offset:
            arrived(buf.at[slot], sem.at[slot])
        for step in steps:
            send(buf.at[slot], buf.at[slot], sem.at[slot], on_ring(step))
        for plane, copy in edges:
            @pl.when(at == plane)
            def _():
                copy.start()

    def pass_x(offset, *steps):
        pass_on(sp, sp_sem, 2, x_edges, offset, steps)

    def others(buf, sem):
        send(buf, buf, sem, (gz, far))
        send(buf, buf, sem, (gz, core))

    def hand_over(buf, sem):
        arrived(buf, sem)
        send(buf, buf, sem, (gz, core))

    def halves(buf, sem, base):
        rows = buf.shape[1] // 2
        for offset, step, first in ((5, 1, 0), (3, 7, rows)):
            slot = base + (z + offset) % 8
            part = buf.at[slot, pl.ds(first, rows)]
            send(part, part, sem.at[slot], on_ring(step))

    pass_x(0, 1, 7)
    for load in other_loads:
        load.wait()
    send(g_ref, gh.at[0], gh_sem.at[0], (above, col))
    send(g_ref, gh.at[1], gh_sem.at[1], (below, col))
    others(xc.at[col, 1], xc_sem.at[col, 1])
    others(gc.at[col], gc_sem.at[col])

    loads[0].wait()
    wt[:, 0:64] = jnp.transpose(w_ref[...].astype(F32))
    wt[:, 64:128] = jnp.zeros((3456, 64), F32)
    for tap in range(TAPS):
        block = wt[pl.ds(tap, 128, stride=TAPS), :]
        wg[:, tap * 64:tap * 64 + 64] = block[:, 0:64].astype(BF)
        wy[:, tap * 128:tap * 128 + 128] = jnp.transpose(block)[0:64].astype(BF)

    pass_x(7, 1)
    pass_x(1, 7)

    entry = lax.broadcasted_iota(jnp.int32, (128, 864), 0)
    column = lax.broadcasted_iota(jnp.int32, (128, 864), 1)
    home = jnp.where(entry < 96, entry % 32 * 27 + entry // 32 * 9, -27)
    for be in range(9):
        column_ref[be * 128:be * 128 + 128, :] = keep(column == home + be)

    cotangent_taps(1, g_ref[...])
    pass_x(6, 1)
    pass_x(2, 7)
    hand_over(xc.at[far, 1], xc_sem.at[far, 1])
    hand_over(gc.at[far], gc_sem.at[far])
    pass_x(5)
    pass_x(3)
    halves(sp, sp_sem, 2)
    for slot, edge in ((0, 0), (1, 63)):
        arrived(gh.at[slot], gh_sem.at[slot])

        @pl.when(gz == edge)
        def _():
            gh[slot] = jnp.zeros((64, YX), BF)

    cotangent_taps(0, gh[1])
    cotangent_taps(2, gh[0])
    arrived(xc.at[core, 1], xc_sem.at[core, 1])
    arrived(xc.at[diag, 1], xc_sem.at[diag, 1])
    grad_w = lax.dot_general(xc[:, 1].reshape(128, YX), gp[...], NT, preferred_element_type=F32)
    for kj in range(8):
        mg[kj % 4, kj // 4, :, 0:1728] = grad_w[16 * kj:16 * kj + 16]
        mg[kj % 4, kj // 4, :, 1728:1792] = jnp.zeros((16, 64), F32)
    arrived(gc.at[core], gc_sem.at[core])
    arrived(gc.at[diag], gc_sem.at[diag])
    gram = lax.dot_general(gc[...].reshape(256, YX), g_ref[...], NT, preferred_element_type=F32)
    for kj in range(8):
        mg[kj % 4, kj // 4, :, 1792:1856] = gram[32 * kj:32 * kj + 16]
        mg[kj % 4, kj // 4, :, 1856:1920] = gram[32 * kj + 16:32 * kj + 32]
    for step in (1, 2, 3):
        to = (yk + step) % 4
        send(mg.at[to], rg.at[yk], rg_sem.at[yk], ((xl * 4 + to) * 8 + z, col))

    pass_x(4)

    pick = lax.broadcasted_iota(jnp.int32, (32, 256), 0)
    source = lax.broadcasted_iota(jnp.int32, (32, 256), 1)
    wanted = pick // 4 * 32 + pick // 2 % 2 * 16 + 2 * z + pick % 2
    r4[col] = jnp.dot(keep(source == wanted), sp[2:10].reshape(256, YX), preferred_element_type=F32).astype(BF)
    others(r4.at[col], r4_sem.at[col])

    gi[...] = jnp.dot(wg[...], gp[...], preferred_element_type=F32).reshape(4, 32, YX)
    send(gi.at[core], rgi.at[0], gi_sem.at[0], (gz, core))
    send(gi.at[diag], rgi.at[1], gi_sem.at[1], (gz, core))
    hand_over(r4.at[far], r4_sem.at[far])
    for buf, sem, slot, edge in ((sp, sp_sem, 0, 0), (sp, sp_sem, 1, 0), (sp, sp_sem, 10, 7), (sp, sp_sem, 11, 7)):
        arrived(buf.at[slot], sem.at[slot])

        @pl.when(k == edge)
        def _():
            buf[slot] = jnp.zeros(buf.shape[1:], BF)

    for side in (0, 2):
        xc[col, side] = sp[1 + z + side]
        others(xc.at[col, side], xc_sem.at[col, side])

    arrived(rgi.at[1], gi_sem.at[1])
    up[...] = gi[far] + rgi[1]
    send(up, rgi.at[2], gi_sem.at[2], (gz, far))
    arrived(r4.at[core], r4_sem.at[core])
    arrived(r4.at[diag], r4_sem.at[diag])
    rp[...] = jnp.dot(
        order_ref[...], r4[...].reshape(128, YX), preferred_element_type=F32).astype(BF).reshape(8, 16, YX)

    da[...] = jnp.zeros((784, 128), F32)
    db[...] = jnp.zeros((800, 128), F32)
    edge_plane = jnp.where(k < 4, 0, 7)

    def variants(value, unit, at, size):
        out = []
        for delta in (-2, -1, 0, 1, 2):
            inside = jnp.logical_and(at - delta >= 0, at - delta < size)
            out.append(value if delta == 0 else moved(value, -delta * unit) * keep(inside))
        out.append(value * keep(at >= 1))
        out.append(value * keep(at < size - 1))
        return out

    def factor_plane(v):
        rows = rp[v]
        for tx, line in enumerate(variants(rows, 1, place, SIDE)):
            for ty, plane in enumerate(variants(line, SIDE, row, SIDE)):
                at = (ty * 7 + tx) * 16
                rv[at:at + 16, :] = plane
        beside = sp[pl.ds(v, 5)].reshape(160, YX)
        flag = jnp.where(v == edge_plane, 1.0, 0.0).astype(BF)
        columns = jnp.concatenate([beside, sp[v + 2] * flag], axis=0)
        part = lax.dot_general(rv[...], columns, NT, preferred_element_type=F32)
        da[...] += part[:, 0:128]
        db[0:784, 0:64] += part[:, 128:192]

    @pl.loop(0, 8)
    def _(v):
        factor_plane(v)

    for step in (1, 2, 3):
        slot = (yk + step) % 4
        arrived(rg.at[slot], rg_sem.at[slot])
    mx[1] = mg[yk, 1 - xl] + rg[(yk + 1) % 4, 1 - xl] + rg[(yk + 2) % 4, 1 - xl] + rg[(yk + 3) % 4, 1 - xl]
    send(mx.at[1], rx, rx_sem.at[0], (((1 - xl) * 4 + yk) * 8 + z, col))
    mx[0] = mg[yk, xl] + rg[(yk + 1) % 4, xl] + rg[(yk + 2) % 4, xl] + rg[(yk + 3) % 4, xl]

    lane = lax.broadcasted_iota(jnp.int32, (25, 128), 1)

    def packed(kj, first):
        out = None
        for q in range(4):
            run = db[pl.ds(2 * kj + q // 2 + 400 * (q % 2), 25, stride=16), :]
            step = (32 * q - first) % 128
            run = pltpu.roll(run, shift=step, axis=1) if step else run
            out = run if out is None else jnp.where(lane // 32 == q, run, out)
        return out

    for kj in range(8):
        for p in range(2):
            mp[kj, 49 * p:49 * p + 49] = da[pl.ds(2 * kj + p, 49, stride=16), :]
        mp[kj, 98:123] = packed(kj, 0)
    for kj in peers:
        send(mp.at[kj], rpf.at[k], rpf_sem.at[k], (kj * 8 + z, col))
    def face_copies(owner):
        return [pltpu.make_async_remote_copy(
            src_ref=me.at[(owner + j) % 8], dst_ref=re.at[owner // 7], send_sem=late_sem.at[24 + j],
            recv_sem=re_sem.at[owner // 7], device_id=((owner + j) % 8 * 8 + z, col),
            device_id_type=MESH) for j in range(1, 8)]

    for owner in (0, 7):
        @pl.when(k == owner)
        def _():
            for kj in range(8):
                me[kj] = packed(kj, 32)
            for copy in face_copies(owner):
                copy.start()
            re[owner // 7] = me[owner]

    arrived(rx, rx_sem.at[0])
    total = mx[0] + rx[...]
    for j in range(14):
        for zj in range(8):
            b3[zj, 2 * j:2 * j + 2, :] = total[2 * zj:2 * zj + 2, 128 * j:128 * j + 128]
    sides = (total[:, 1792:1920], pltpu.roll(total[:, 1792:1920], shift=64, axis=1))
    for zj in range(8):
        b3[zj, 28:32, :] = sides[zj // 4][4 * (zj % 4):4 * (zj % 4) + 4]
    for zj in ring:
        send(b3.at[zj], rb.at[z], rb_sem.at[z], (k * 8 + zj, col))

    for side in (0, 2):
        hand_over(xc.at[far, side], xc_sem.at[far, side])

    for side in (0, 2):
        arrived(xc.at[core, side], xc_sem.at[core, side])
        arrived(xc.at[diag, side], xc_sem.at[diag, side])

    for a in range(3):
        plane = xc[:, a].reshape(128, YX)
        for e in range(3):
            line = shifted(plane, 0, e - 1)
            for b in range(3):
                tap = 9 * a + 3 * b + e
                xp[tap * 128:(tap + 1) * 128, :] = shifted(line, b - 1, 0)
    y_ref[0] = jnp.dot(wy[...], xp[...], preferred_element_type=F32).astype(BF)

    arrived(rgi.at[0], gi_sem.at[0])
    arrived(rgi.at[2], gi_sem.at[2])
    gi_ref[0] = (gi[col] + rgi[0] + rgi[2]).astype(BF)

    total = mp[k]
    for kj in peers:
        arrived(rpf.at[kj], rpf_sem.at[kj])
        total = total + rpf[kj]
    for owner in (0, 7):
        @pl.when(k != owner)
        def _():
            arrived(re.at[owner // 7], re_sem.at[owner // 7])
    low, high = re[0], re[1]
    pad = jnp.zeros((49, 32), F32)

    def unpacked(value, p):
        at = 64 * p
        return jnp.concatenate([value[0:25, at:at + 32], value[0:24, at + 32:at + 64]], axis=0)

    for p in range(2):
        head = total[49 * p:49 * p + 49]
        m2, m1, zero, p1 = [head[:, 32 * i:32 * i + 32] for i in range(4)]
        p2 = unpacked(total[98:123], p)
        first, last = unpacked(low, p), unpacked(high, p)
        wide = jnp.concatenate(
            [zero - last, p1, p2, pad, m1, zero, p1, pad, m2, m1, zero - first, pad], axis=1)
        for part in range(3):
            piece = wide.astype(BF)
            wide = wide - piece.astype(F32)
            picked = jnp.dot(choice_ref[...], piece, preferred_element_type=F32).astype(BF)
            for a in range(3):
                at = (part * 6 + p * 3 + a) * 16
                for be in range(9):
                    lh[at:at + 16, be * 128:be * 128 + 128] = picked[be * 16:be * 16 + 16, a * 128:a * 128 + 128]
    factor = jnp.dot(lh[...], column_ref[...], preferred_element_type=F32)
    factor = (factor[0:96] + factor[96:192] + factor[192:288]) * (1.0 / 65536)
    for block in range(6):
        pf_ref[block * 9:block * 9 + 9, :] = factor[block * 16:block * 16 + 9]

    total = b3[z]
    for zj in ring:
        arrived(rb.at[zj], rb_sem.at[zj])
        total = total + rb[zj]
    gf_ref[...] = total[28:32, 0:64] * (1.0 / 65536)
    for tap in range(TAPS):
        for p in range(2):
            at = 2 * (tap // 2) + p
            gw_ref[p * 27 + tap:p * 27 + tap + 1, :] = total[at:at + 1, 64 * (tap % 2):64 * (tap % 2) + 64] * (1.0 / 256)

    for _, copy in x_edges:
        copy.wait_send()
    for copy in sends:
        copy.wait_send()
    for owner in (0, 7):
        @pl.when(k == owner)
        def _():
            for copy in face_copies(owner):
                copy.wait_send()


def deliver(*refs):
    for i in range(5):
        refs[5 + i][...] = refs[i][...]


def shards(x_field, weights, grad_out):
    vmem = pl.BlockSpec(memory_space=pltpu.VMEM)
    there = pl.BlockSpec(memory_space=pl.ANY)
    dma = pltpu.SemaphoreType.DMA
    shapes = (
        jax.ShapeDtypeStruct((1, 64, YX), BF),
        jax.ShapeDtypeStruct((1, 32, YX), BF),
        jax.ShapeDtypeStruct((54, 64), F32),
        jax.ShapeDtypeStruct((54, 864), F32),
        jax.ShapeDtypeStruct((4, 64), F32),
    )
    results = pl.pallas_call(
        kernel,
        out_shape=shapes,
        in_specs=[there] * 5,
        out_specs=(vmem,) * 5,
        scratch_shapes=[
            pltpu.VMEM((64, YX), BF),
            pltpu.VMEM((64, 3456), BF),
            pltpu.VMEM((128, 128), BF),
            pltpu.VMEM((144, 49), BF),
            pltpu.VMEM((1152, 864), BF),
            pltpu.VMEM((3456, 128), F32),
            pltpu.VMEM((64, 3456), BF),
            pltpu.VMEM((128, 1728), BF),
            pltpu.VMEM((4, 3, 32, YX), BF),
            pltpu.VMEM((4, 64, YX), BF),
            pltpu.VMEM((2, 64, YX), BF),
            pltpu.VMEM((12, 32, YX), BF),
            pltpu.VMEM((4, 32, YX), BF),
            pltpu.VMEM((8, 16, YX), BF),
            pltpu.VMEM((3456, YX), BF),
            pltpu.VMEM((1728, YX), BF),
            pltpu.VMEM((784, YX), BF),
            pltpu.VMEM((784, 128), F32),
            pltpu.VMEM((800, 128), F32),
            pltpu.VMEM((4, 2, 16, 1920), F32),
            pltpu.VMEM((4, 2, 16, 1920), F32),
            pltpu.VMEM((2, 16, 1920), F32),
            pltpu.VMEM((16, 1920), F32),
            pltpu.VMEM((8, 32, 128), F32),
            pltpu.VMEM((8, 32, 128), F32),
            pltpu.VMEM((8, 123, 128), F32),
            pltpu.VMEM((8, 123, 128), F32),
            pltpu.VMEM((8, 25, 128), F32),
            pltpu.VMEM((2, 25, 128), F32),
            pltpu.VMEM((4, 32, YX), F32),
            pltpu.VMEM((3, 32, YX), F32),
            pltpu.VMEM((32, YX), F32),
            pltpu.VMEM((288, 1152), BF),
            dma((72,)),
            dma((32,)),
            dma((8,)),
            dma((4, 3)),
            dma((4,)),
            dma((2,)),
            dma((12,)),
            dma((4,)),
            dma((4,)),
            dma((1,)),
            dma((8,)),
            dma((8,)),
            dma((2,)),
            dma((3,)),
        ],
        compiler_params=pltpu.CompilerParams(
            collective_id=0, has_side_effects=True, vmem_limit_bytes=56 * 2**20),
    )(x_field, grad_out, weights,
      jnp.asarray(channel_order(), BF), jnp.asarray(type_choice(), BF))
    return pl.pallas_call(
        deliver,
        out_shape=shapes,
        in_specs=[vmem] * 5,
        out_specs=(vmem,) * 5,
    )(*results)


def solution(mesh):
    return jax.shard_map(
        shards,
        mesh=mesh,
        in_specs=(P("gz", "col", None), P("col", None), P("gz", "col", None)),
        out_specs=(
            P("gz", "col", None),
            P("gz", "col", None),
            P("gz", "col"),
            P("gz", "col"),
            P("gz", "col"),
        ),
        check_vma=False,
    )
```

```python
import jax
import jax.numpy as jnp
import numpy as np
from jax import lax
from jax.experimental import pallas as pl
from jax.experimental.pallas import tpu as pltpu
from jax.sharding import PartitionSpec as P

MESH = pl.DeviceIdType.MESH
BF, F32 = jnp.bfloat16, jnp.float32
SIDE, YX, TAPS = 32, 1024, 27
NT = (((1,), (1,)), ((), ()))


def kind(first, second):
    if first != second:
        return second - first + 2
    return {1: 2, 2: 5, 0: 6}[first]


def channel_order():
    out = np.zeros((128, 128), np.float32)
    for v in range(8):
        for k in range(8):
            for p in range(2):
                out[v * 16 + 2 * k + p, k // 2 * 32 + v * 4 + 2 * (k % 2) + p] = 1
    return out


def type_choice():
    out = np.zeros((144, 49), np.float32)
    for b2 in range(3):
        for e2 in range(3):
            for b in range(3):
                for e in range(3):
                    out[(b2 * 3 + e2) * 16 + b * 3 + e, kind(b, b2) * 7 + kind(e, e2)] = 1
    return out


def moved(value, step):
    step = step % YX
    return value if step == 0 else pltpu.roll(value, shift=(YX - step) % YX, axis=1)


def cell_masks():
    cell = lax.broadcasted_iota(jnp.int32, (1, YX), 1)
    return cell // SIDE, cell % SIDE


def keep(where):
    return where.astype(F32).astype(BF)


def kernel(x_hbm, g_hbm, w_hbm, order_hbm, choice_hbm,
           y_ref, gi_ref, gw_ref, pf_ref, gf_ref,
           g_ref, w_ref, order_ref, choice_ref, column_ref, wt, wy, wg,
           xc, gc, gh, sp, r4, rp, xp, gp, rv, da, db, mg, rg, mx, rx, ng, nx, nt, ny, b3, rb, mp, rpf, me, re, gi, rgi, up, lh,
           send_sem, late_sem, load_sem, xc_sem, gc_sem, gh_sem, sp_sem, r4_sem, rg_sem, rx_sem, nx_sem, ny_sem, rb_sem, rpf_sem, re_sem,
           gi_sem):
    gz, col = lax.axis_index("gz"), lax.axis_index("col")
    k, z = gz // 8, gz % 8
    core = col + 1 - 2 * (col % 2)
    far = (col + 2) % 4
    diag = (core + 2) % 4
    ring = [(z + j) % 8 for j in (1, 7, 2, 6, 3, 5, 4)]
    peers = [(k + j) % 8 for j in range(1, 8)]
    x_own, g_own = x_hbm.at[0], g_hbm.at[0]

    def on_ring(offset):
        return (k * 8 + (z + offset) % 8, col)

    sends = []

    def send(src, dst, sem, target):
        copy = pltpu.make_async_remote_copy(
            src_ref=src, dst_ref=dst, send_sem=send_sem.at[len(sends)], recv_sem=sem,
            device_id=target, device_id_type=MESH)
        copy.start()
        sends.append(copy)

    def arrived(dst, sem):
        pltpu.make_async_remote_copy(
            src_ref=dst, dst_ref=dst, send_sem=send_sem.at[0], recv_sem=sem,
            device_id=(gz, core), device_id_type=MESH).wait_recv()

    barrier = pltpu.get_barrier_semaphore()
    above, below = (gz + 1) % 64, (gz + 63) % 64
    xl, yk = k // 4, k % 4
    partners = [(gz, core), (gz, far), (above, col), (below, col)]
    partners += [(k * 8 + zj, col) for zj in ring] + [(kj * 8 + z, col) for kj in peers]
    for target in partners:
        pl.semaphore_signal(barrier, inc=1, device_id=target, device_id_type=MESH)
    loads = [pltpu.make_async_copy(src, dst, load_sem.at[i]) for i, (src, dst) in enumerate((
        (w_hbm, w_ref), (g_own, g_ref), (x_own, xc.at[col, 1]), (x_own, sp.at[2 + z]), (g_own, gc.at[col]),
        (order_hbm, order_ref), (choice_hbm, choice_ref)))]
    for load in loads:
        load.start()
    row, place = cell_masks()
    in_row = {-1: keep(place >= 1), 1: keep(place < SIDE - 1)}
    in_plane = {-1: keep(row >= 1), 1: keep(row < SIDE - 1)}

    def shifted(value, dy, dx):
        if dx:
            value = moved(value, dx) * in_row[dx]
        if dy:
            value = moved(value, SIDE * dy) * in_plane[dy]
        return value

    def cotangent_taps(a, plane):
        for e in range(3):
            line = shifted(plane, 0, 1 - e)
            for b in range(3):
                tap = 9 * a + 3 * b + e
                gp[tap * 64:(tap + 1) * 64, :] = shifted(line, 1 - b, 0)

    x_loads, other_loads = loads[2:4], loads[1:2] + loads[4:]
    for load in x_loads:
        load.wait()
    pl.semaphore_wait(barrier, len(partners))

    x_edges = [(plane, pltpu.make_async_remote_copy(
        src_ref=sp.at[2 + plane], dst_ref=sp.at[home], send_sem=late_sem.at[late], recv_sem=sp_sem.at[home, 0],
        device_id=((k + step) % 8 * 8 + z, col), device_id_type=MESH))
        for late, (plane, home, step) in enumerate(((0, 10, 7), (1, 11, 7), (6, 0, 1), (7, 1, 1)))]

    def half(offset, part):
        slot = 2 + (z + offset) % 8
        return sp.at[slot, pl.ds(16 * part, 16)], sp_sem.at[slot, part]

    def take(offset, part):
        arrived(*half(offset, part))

    def give(offset, part, step):
        rows, sem = half(offset, part)
        send(rows, rows, sem, on_ring(step))

    def pass_on(up, down):
        for part in (0, 1):
            if up:
                take(up, part)
            give(up, part, 1)
            if down:
                take(down, 1 - part)
            give(down, 1 - part, 7)

    def outward(*offsets):
        for offset in offsets:
            for plane, copy in x_edges:
                @pl.when((z + offset) % 8 == plane)
                def _():
                    copy.start()

    def others(buf, sem):
        send(buf, buf, sem, (gz, far))
        send(buf, buf, sem, (gz, core))

    def hand_over(buf, sem):
        arrived(buf, sem)
        send(buf, buf, sem, (gz, core))

    pass_on(0, 0)
    outward(0)
    for load in other_loads:
        load.wait()
    send(g_ref, gh.at[0], gh_sem.at[0], (above, col))
    send(g_ref, gh.at[1], gh_sem.at[1], (below, col))
    others(xc.at[col, 1], xc_sem.at[col, 1])
    others(gc.at[col], gc_sem.at[col])

    loads[0].wait()
    wt[:, 0:64] = jnp.transpose(w_ref[...].astype(F32))
    wt[:, 64:128] = jnp.zeros((3456, 64), F32)
    for tap in range(TAPS):
        block = wt[pl.ds(tap, 128, stride=TAPS), :]
        wg[:, tap * 64:tap * 64 + 64] = block[:, 0:64].astype(BF)
        wy[:, tap * 128:tap * 128 + 128] = jnp.transpose(block)[0:64].astype(BF)

    pass_on(7, 1)
    outward(7, 1)

    cotangent_taps(1, g_ref[...])
    pass_on(6, 2)
    outward(6, 2)
    hand_over(xc.at[far, 1], xc_sem.at[far, 1])
    for slot, edge in ((0, 0), (1, 63)):
        arrived(gh.at[slot], gh_sem.at[slot])

        @pl.when(gz == edge)
        def _():
            gh[slot] = jnp.zeros((64, YX), BF)

    cotangent_taps(0, gh[1])
    cotangent_taps(2, gh[0])
    take(5, 0)
    give(5, 0, 1)
    take(3, 1)
    give(3, 1, 7)
    take(5, 1)
    take(3, 0)
    outward(5, 3)
    arrived(xc.at[core, 1], xc_sem.at[core, 1])
    arrived(xc.at[diag, 1], xc_sem.at[diag, 1])
    grad_w = lax.dot_general(xc[:, 1].reshape(128, YX), gp[...], NT, preferred_element_type=F32)
    take(4, 0)
    take(4, 1)
    outward(4)

    pick = lax.broadcasted_iota(jnp.int32, (32, 256), 0)
    source = lax.broadcasted_iota(jnp.int32, (32, 256), 1)
    wanted = pick // 4 * 32 + pick // 2 % 2 * 16 + 2 * z + pick % 2
    r4[col] = jnp.dot(keep(source == wanted), sp[2:10].reshape(256, YX), preferred_element_type=F32).astype(BF)
    others(r4.at[col], r4_sem.at[col])
    hand_over(gc.at[far], gc_sem.at[far])

    for kj in range(8):
        mg[kj % 4, kj // 4] = grad_w[16 * kj:16 * kj + 16, 0:1280]
        ng[kj // 4, kj % 4, :, 0:448] = grad_w[16 * kj:16 * kj + 16, 1280:1728]
        ng[kj // 4, kj % 4, :, 448:512] = jnp.zeros((16, 64), F32)
    arrived(gc.at[core], gc_sem.at[core])
    arrived(gc.at[diag], gc_sem.at[diag])
    gram = lax.dot_general(gc[...].reshape(256, YX), g_ref[...], NT, preferred_element_type=F32)
    for kj in range(8):
        ng[kj // 4, kj % 4, :, 512:576] = gram[32 * kj:32 * kj + 16]
        ng[kj // 4, kj % 4, :, 576:640] = gram[32 * kj + 16:32 * kj + 32]
    send(ng.at[1 - xl], nx, nx_sem.at[0], (((1 - xl) * 4 + yk) * 8 + z, col))
    for step in (1, 2, 3):
        to = (yk + step) % 4
        send(mg.at[to], rg.at[yk], rg_sem.at[yk], ((xl * 4 + to) * 8 + z, col))


    entry = lax.broadcasted_iota(jnp.int32, (128, 864), 0)
    column = lax.broadcasted_iota(jnp.int32, (128, 864), 1)
    home = jnp.where(entry < 96, entry % 32 * 27 + entry // 32 * 9, -27)
    for be in range(9):
        column_ref[be * 128:be * 128 + 128, :] = keep(column == home + be)

    gi[...] = jnp.dot(wg[...], gp[...], preferred_element_type=F32).reshape(4, 32, YX)
    send(gi.at[core], rgi.at[0], gi_sem.at[0], (gz, core))
    send(gi.at[diag], rgi.at[1], gi_sem.at[1], (gz, core))
    hand_over(r4.at[far], r4_sem.at[far])
    for slot, edge in ((0, 0), (1, 0), (10, 7), (11, 7)):
        arrived(sp.at[slot], sp_sem.at[slot, 0])

        @pl.when(k == edge)
        def _():
            sp[slot] = jnp.zeros((32, YX), BF)

    for side in (0, 2):
        xc[col, side] = sp[1 + z + side]
        others(xc.at[col, side], xc_sem.at[col, side])

    arrived(rgi.at[1], gi_sem.at[1])
    up[...] = gi[far] + rgi[1]
    send(up, rgi.at[2], gi_sem.at[2], (gz, far))
    arrived(r4.at[core], r4_sem.at[core])
    arrived(r4.at[diag], r4_sem.at[diag])
    rp[...] = jnp.dot(
        order_ref[...], r4[...].reshape(128, YX), preferred_element_type=F32).astype(BF).reshape(8, 16, YX)

    da[...] = jnp.zeros((784, 128), F32)
    db[...] = jnp.zeros((800, 128), F32)
    edge_plane = jnp.where(k < 4, 0, 7)

    def variants(value, unit, at, size):
        out = []
        for delta in (-2, -1, 0, 1, 2):
            inside = jnp.logical_and(at - delta >= 0, at - delta < size)
            out.append(value if delta == 0 else moved(value, -delta * unit) * keep(inside))
        out.append(value * keep(at >= 1))
        out.append(value * keep(at < size - 1))
        return out

    def factor_plane(v):
        rows = rp[v]
        for tx, line in enumerate(variants(rows, 1, place, SIDE)):
            for ty, plane in enumerate(variants(line, SIDE, row, SIDE)):
                at = (ty * 7 + tx) * 16
                rv[at:at + 16, :] = plane
        beside = sp[pl.ds(v, 5)].reshape(160, YX)
        flag = jnp.where(v == edge_plane, 1.0, 0.0).astype(BF)
        columns = jnp.concatenate([beside, sp[v + 2] * flag], axis=0)
        part = lax.dot_general(rv[...], columns, NT, preferred_element_type=F32)
        da[...] += part[:, 0:128]
        db[0:784, 0:64] += part[:, 128:192]

    @pl.loop(0, 5)
    def _(v):
        factor_plane(v)

    arrived(nx, nx_sem.at[0])
    nt[...] = ng[xl] + nx[...]
    for step in (1, 2, 3):
        to = (yk + step) % 4
        send(nt.at[to], ny.at[yk], ny_sem.at[yk], ((xl * 4 + to) * 8 + z, col))

    @pl.loop(5, 8)
    def _(v):
        factor_plane(v)

    for step in (1, 2, 3):
        slot = (yk + step) % 4
        arrived(rg.at[slot], rg_sem.at[slot])
    mx[1] = mg[yk, 1 - xl] + rg[(yk + 1) % 4, 1 - xl] + rg[(yk + 2) % 4, 1 - xl] + rg[(yk + 3) % 4, 1 - xl]
    send(mx.at[1], rx, rx_sem.at[0], (((1 - xl) * 4 + yk) * 8 + z, col))
    mx[0] = mg[yk, xl] + rg[(yk + 1) % 4, xl] + rg[(yk + 2) % 4, xl] + rg[(yk + 3) % 4, xl]

    lane = lax.broadcasted_iota(jnp.int32, (25, 128), 1)

    def packed(kj, first):
        out = None
        for q in range(4):
            run = db[pl.ds(2 * kj + q // 2 + 400 * (q % 2), 25, stride=16), :]
            step = (32 * q - first) % 128
            run = pltpu.roll(run, shift=step, axis=1) if step else run
            out = run if out is None else jnp.where(lane // 32 == q, run, out)
        return out

    for kj in range(8):
        for p in range(2):
            mp[kj, 49 * p:49 * p + 49] = da[pl.ds(2 * kj + p, 49, stride=16), :]
        mp[kj, 98:123] = packed(kj, 0)
    for kj in peers:
        send(mp.at[kj], rpf.at[k], rpf_sem.at[k], (kj * 8 + z, col))
    def face_copies(owner):
        return [pltpu.make_async_remote_copy(
            src_ref=me.at[(owner + j) % 8], dst_ref=re.at[owner // 7], send_sem=late_sem.at[24 + j],
            recv_sem=re_sem.at[owner // 7], device_id=((owner + j) % 8 * 8 + z, col),
            device_id_type=MESH) for j in range(1, 8)]

    for owner in (0, 7):
        @pl.when(k == owner)
        def _():
            for kj in range(8):
                me[kj] = packed(kj, 32)
            for copy in face_copies(owner):
                copy.start()
            re[owner // 7] = me[owner]

    arrived(rx, rx_sem.at[0])
    early = mx[0] + rx[...]
    late = nt[yk]
    for step in (1, 2, 3):
        slot = (yk + step) % 4
        arrived(ny.at[slot], ny_sem.at[slot])
        late = late + ny[slot]
    tiles = [early[:, 128 * j:128 * j + 128] for j in range(10)] + [late[:, 128 * j:128 * j + 128] for j in range(5)]
    for j in range(14):
        for zj in range(8):
            b3[zj, 2 * j:2 * j + 2, :] = tiles[j][2 * zj:2 * zj + 2]
    sides = (tiles[14], pltpu.roll(tiles[14], shift=64, axis=1))
    for zj in range(8):
        b3[zj, 28:32, :] = sides[zj // 4][4 * (zj % 4):4 * (zj % 4) + 4]
    for zj in ring:
        send(b3.at[zj], rb.at[z], rb_sem.at[z], (k * 8 + zj, col))

    for side in (0, 2):
        hand_over(xc.at[far, side], xc_sem.at[far, side])

    for side in (0, 2):
        arrived(xc.at[core, side], xc_sem.at[core, side])
        arrived(xc.at[diag, side], xc_sem.at[diag, side])

    for a in range(3):
        plane = xc[:, a].reshape(128, YX)
        for e in range(3):
            line = shifted(plane, 0, e - 1)
            for b in range(3):
                tap = 9 * a + 3 * b + e
                xp[tap * 128:(tap + 1) * 128, :] = shifted(line, b - 1, 0)
    y_ref[0] = jnp.dot(wy[...], xp[...], preferred_element_type=F32).astype(BF)

    arrived(rgi.at[0], gi_sem.at[0])
    arrived(rgi.at[2], gi_sem.at[2])
    gi_ref[0] = (gi[col] + rgi[0] + rgi[2]).astype(BF)

    total = mp[k]
    for kj in peers:
        arrived(rpf.at[kj], rpf_sem.at[kj])
        total = total + rpf[kj]
    for owner in (0, 7):
        @pl.when(k != owner)
        def _():
            arrived(re.at[owner // 7], re_sem.at[owner // 7])
    low, high = re[0], re[1]
    pad = jnp.zeros((49, 32), F32)

    def unpacked(value, p):
        at = 64 * p
        return jnp.concatenate([value[0:25, at:at + 32], value[0:24, at + 32:at + 64]], axis=0)

    for p in range(2):
        head = total[49 * p:49 * p + 49]
        m2, m1, zero, p1 = [head[:, 32 * i:32 * i + 32] for i in range(4)]
        p2 = unpacked(total[98:123], p)
        first, last = unpacked(low, p), unpacked(high, p)
        wide = jnp.concatenate(
            [zero - last, p1, p2, pad, m1, zero, p1, pad, m2, m1, zero - first, pad], axis=1)
        for part in range(3):
            piece = wide.astype(BF)
            wide = wide - piece.astype(F32)
            picked = jnp.dot(choice_ref[...], piece, preferred_element_type=F32).astype(BF)
            for a in range(3):
                at = (part * 6 + p * 3 + a) * 16
                for be in range(9):
                    lh[at:at + 16, be * 128:be * 128 + 128] = picked[be * 16:be * 16 + 16, a * 128:a * 128 + 128]
    factor = jnp.dot(lh[...], column_ref[...], preferred_element_type=F32)
    factor = (factor[0:96] + factor[96:192] + factor[192:288]) * (1.0 / 65536)
    for block in range(6):
        pf_ref[block * 9:block * 9 + 9, :] = factor[block * 16:block * 16 + 9]

    total = b3[z]
    for zj in ring:
        arrived(rb.at[zj], rb_sem.at[zj])
        total = total + rb[zj]
    gf_ref[...] = total[28:32, 0:64] * (1.0 / 65536)
    for tap in range(TAPS):
        for p in range(2):
            at = 2 * (tap // 2) + p
            gw_ref[p * 27 + tap:p * 27 + tap + 1, :] = total[at:at + 1, 64 * (tap % 2):64 * (tap % 2) + 64] * (1.0 / 256)

    for _, copy in x_edges:
        copy.wait_send()
    for copy in sends:
        copy.wait_send()
    for owner in (0, 7):
        @pl.when(k == owner)
        def _():
            for copy in face_copies(owner):
                copy.wait_send()


def deliver(*refs):
    for i in range(5):
        refs[5 + i][...] = refs[i][...]


def shards(x_field, weights, grad_out):
    vmem = pl.BlockSpec(memory_space=pltpu.VMEM)
    there = pl.BlockSpec(memory_space=pl.ANY)
    dma = pltpu.SemaphoreType.DMA
    shapes = (
        jax.ShapeDtypeStruct((1, 64, YX), BF),
        jax.ShapeDtypeStruct((1, 32, YX), BF),
        jax.ShapeDtypeStruct((54, 64), F32),
        jax.ShapeDtypeStruct((54, 864), F32),
        jax.ShapeDtypeStruct((4, 64), F32),
    )
    results = pl.pallas_call(
        kernel,
        out_shape=shapes,
        in_specs=[there] * 5,
        out_specs=(vmem,) * 5,
        scratch_shapes=[
            pltpu.VMEM((64, YX), BF),
            pltpu.VMEM((64, 3456), BF),
            pltpu.VMEM((128, 128), BF),
            pltpu.VMEM((144, 49), BF),
            pltpu.VMEM((1152, 864), BF),
            pltpu.VMEM((3456, 128), F32),
            pltpu.VMEM((64, 3456), BF),
            pltpu.VMEM((128, 1728), BF),
            pltpu.VMEM((4, 3, 32, YX), BF),
            pltpu.VMEM((4, 64, YX), BF),
            pltpu.VMEM((2, 64, YX), BF),
            pltpu.VMEM((12, 32, YX), BF),
            pltpu.VMEM((4, 32, YX), BF),
            pltpu.VMEM((8, 16, YX), BF),
            pltpu.VMEM((3456, YX), BF),
            pltpu.VMEM((1728, YX), BF),
            pltpu.VMEM((784, YX), BF),
            pltpu.VMEM((784, 128), F32),
            pltpu.VMEM((800, 128), F32),
            pltpu.VMEM((4, 2, 16, 1280), F32),
            pltpu.VMEM((4, 2, 16, 1280), F32),
            pltpu.VMEM((2, 16, 1280), F32),
            pltpu.VMEM((16, 1280), F32),
            pltpu.VMEM((2, 4, 16, 640), F32),
            pltpu.VMEM((4, 16, 640), F32),
            pltpu.VMEM((4, 16, 640), F32),
            pltpu.VMEM((4, 16, 640), F32),
            pltpu.VMEM((8, 32, 128), F32),
            pltpu.VMEM((8, 32, 128), F32),
            pltpu.VMEM((8, 123, 128), F32),
            pltpu.VMEM((8, 123, 128), F32),
            pltpu.VMEM((8, 25, 128), F32),
            pltpu.VMEM((2, 25, 128), F32),
            pltpu.VMEM((4, 32, YX), F32),
            pltpu.VMEM((3, 32, YX), F32),
            pltpu.VMEM((32, YX), F32),
            pltpu.VMEM((288, 1152), BF),
            dma((72,)),
            dma((32,)),
            dma((8,)),
            dma((4, 3)),
            dma((4,)),
            dma((2,)),
            dma((12, 2)),
            dma((4,)),
            dma((4,)),
            dma((1,)),
            dma((1,)),
            dma((4,)),
            dma((8,)),
            dma((8,)),
            dma((2,)),
            dma((3,)),
        ],
        compiler_params=pltpu.CompilerParams(
            collective_id=0, has_side_effects=True, vmem_limit_bytes=56 * 2**20),
    )(x_field, grad_out, weights,
      jnp.asarray(channel_order(), BF), jnp.asarray(type_choice(), BF))
    return pl.pallas_call(
        deliver,
        out_shape=shapes,
        in_specs=[vmem] * 5,
        out_specs=(vmem,) * 5,
    )(*results)


def solution(mesh):
    return jax.shard_map(
        shards,
        mesh=mesh,
        in_specs=(P("gz", "col", None), P("col", None), P("gz", "col", None)),
        out_specs=(
            P("gz", "col", None),
            P("gz", "col", None),
            P("gz", "col"),
            P("gz", "col"),
            P("gz", "col"),
        ),
        check_vma=False,
    )
```

```python
import jax
import jax.numpy as jnp
import numpy as np
from jax import lax
from jax.experimental import pallas as pl
from jax.experimental.pallas import tpu as pltpu
from jax.sharding import PartitionSpec as P

MESH = pl.DeviceIdType.MESH
BF, F32 = jnp.bfloat16, jnp.float32
SIDE, YX, TAPS = 32, 1024, 27
NT = (((1,), (1,)), ((), ()))


def kind(first, second):
    if first != second:
        return second - first + 2
    return {1: 2, 2: 5, 0: 6}[first]


def channel_order():
    out = np.zeros((128, 128), np.float32)
    for v in range(8):
        for k in range(8):
            for p in range(2):
                out[v * 16 + 2 * k + p, k // 2 * 32 + v * 4 + 2 * (k % 2) + p] = 1
    return out


def type_choice():
    out = np.zeros((144, 49), np.float32)
    for b2 in range(3):
        for e2 in range(3):
            for b in range(3):
                for e in range(3):
                    out[(b2 * 3 + e2) * 16 + b * 3 + e, kind(b, b2) * 7 + kind(e, e2)] = 1
    return out


def moved(value, step):
    step = step % YX
    return value if step == 0 else pltpu.roll(value, shift=(YX - step) % YX, axis=1)


def cell_masks():
    cell = lax.broadcasted_iota(jnp.int32, (1, YX), 1)
    return cell // SIDE, cell % SIDE


def keep(where):
    return where.astype(F32).astype(BF)


def kernel(x_hbm, g_hbm, w_hbm, order_hbm, choice_hbm,
           y_ref, gi_ref, gw_ref, pf_ref, gf_ref,
           g_ref, w_ref, order_ref, choice_ref, column_ref, wt, wy, wg,
           xc, gc, gh, sp, r4, rp, xp, gp, rv, da, db, mg, rg, mx, rx, ng, nx, nt, ny, b3, rb, mp, rpf, me, re, gi, rgi, up, lh,
           send_sem, late_sem, load_sem, xc_sem, gc_sem, gh_sem, sp_sem, r4_sem, rg_sem, rx_sem, nx_sem, ny_sem, rb_sem, rpf_sem, re_sem,
           gi_sem):
    gz, col = lax.axis_index("gz"), lax.axis_index("col")
    k, z = gz // 8, gz % 8
    core = col + 1 - 2 * (col % 2)
    far = (col + 2) % 4
    diag = (core + 2) % 4
    ring = [(z + j) % 8 for j in (1, 7, 2, 6, 3, 5, 4)]
    peers = [(k + j) % 8 for j in range(1, 8)]
    x_own, g_own = x_hbm.at[0], g_hbm.at[0]

    def on_ring(offset):
        return (k * 8 + (z + offset) % 8, col)

    sends = []

    def send(src, dst, sem, target):
        copy = pltpu.make_async_remote_copy(
            src_ref=src, dst_ref=dst, send_sem=send_sem.at[len(sends)], recv_sem=sem,
            device_id=target, device_id_type=MESH)
        copy.start()
        sends.append(copy)

    def arrived(dst, sem):
        pltpu.make_async_remote_copy(
            src_ref=dst, dst_ref=dst, send_sem=send_sem.at[0], recv_sem=sem,
            device_id=(gz, core), device_id_type=MESH).wait_recv()

    barrier = pltpu.get_barrier_semaphore()
    above, below = (gz + 1) % 64, (gz + 63) % 64
    xl, yk = k // 4, k % 4
    partners = [(gz, core), (gz, far), (above, col), (below, col)]
    partners += [(k * 8 + zj, col) for zj in ring] + [(kj * 8 + z, col) for kj in peers]
    for target in partners:
        pl.semaphore_signal(barrier, inc=1, device_id=target, device_id_type=MESH)
    loads = [pltpu.make_async_copy(src, dst, load_sem.at[i]) for i, (src, dst) in enumerate((
        (w_hbm, w_ref), (g_own, g_ref), (x_own, xc.at[col, 1]), (x_own, sp.at[2 + z]), (g_own, gc.at[col]),
        (order_hbm, order_ref), (choice_hbm, choice_ref)))]
    for load in loads:
        load.start()
    row, place = cell_masks()
    in_row = {-1: keep(place >= 1), 1: keep(place < SIDE - 1)}
    in_plane = {-1: keep(row >= 1), 1: keep(row < SIDE - 1)}

    def shifted(value, dy, dx):
        if dx:
            value = moved(value, dx) * in_row[dx]
        if dy:
            value = moved(value, SIDE * dy) * in_plane[dy]
        return value

    def cotangent_taps(a, plane):
        for e in range(3):
            line = shifted(plane, 0, 1 - e)
            for b in range(3):
                tap = 9 * a + 3 * b + e
                gp[tap * 64:(tap + 1) * 64, :] = shifted(line, 1 - b, 0)

    x_loads, other_loads = loads[2:4], loads[1:2] + loads[4:]
    for load in x_loads:
        load.wait()
    pl.semaphore_wait(barrier, len(partners))

    x_edges = [(plane, pltpu.make_async_remote_copy(
        src_ref=sp.at[2 + plane], dst_ref=sp.at[home], send_sem=late_sem.at[late], recv_sem=sp_sem.at[home, 0],
        device_id=((k + step) % 8 * 8 + z, col), device_id_type=MESH))
        for late, (plane, home, step) in enumerate(((0, 10, 7), (1, 11, 7), (6, 0, 1), (7, 1, 1)))]

    def half(offset, part):
        slot = 2 + (z + offset) % 8
        return sp.at[slot, pl.ds(16 * part, 16)], sp_sem.at[slot, part]

    def take(offset, part):
        arrived(*half(offset, part))

    def give(offset, part, step):
        rows, sem = half(offset, part)
        send(rows, rows, sem, on_ring(step))

    def pass_on(up, down):
        for part in (0, 1):
            if up:
                take(up, part)
            give(up, part, 1)
            if down:
                take(down, 1 - part)
            give(down, 1 - part, 7)

    def outward(*offsets):
        for offset in offsets:
            for plane, copy in x_edges:
                @pl.when((z + offset) % 8 == plane)
                def _():
                    copy.start()

    def others(buf, sem):
        send(buf, buf, sem, (gz, far))
        send(buf, buf, sem, (gz, core))

    def hand_over(buf, sem):
        arrived(buf, sem)
        send(buf, buf, sem, (gz, core))

    pass_on(0, 0)
    outward(0)
    for load in other_loads:
        load.wait()
    send(g_ref, gh.at[0], gh_sem.at[0], (above, col))
    send(g_ref, gh.at[1], gh_sem.at[1], (below, col))
    others(xc.at[col, 1], xc_sem.at[col, 1])
    others(gc.at[col], gc_sem.at[col])

    loads[0].wait()
    wt[:, 0:64] = jnp.transpose(w_ref[...].astype(F32))
    wt[:, 64:128] = jnp.zeros((3456, 64), F32)
    for tap in range(TAPS):
        block = wt[pl.ds(tap, 128, stride=TAPS), :]
        wg[:, tap * 64:tap * 64 + 64] = block[:, 0:64].astype(BF)
        wy[:, tap * 128:tap * 128 + 128] = jnp.transpose(block)[0:64].astype(BF)

    pass_on(7, 1)
    outward(7, 1)

    cotangent_taps(1, g_ref[...])
    pass_on(6, 2)
    outward(6, 2)
    hand_over(xc.at[far, 1], xc_sem.at[far, 1])
    for slot, edge in ((0, 0), (1, 63)):
        arrived(gh.at[slot], gh_sem.at[slot])

        @pl.when(gz == edge)
        def _():
            gh[slot] = jnp.zeros((64, YX), BF)

    cotangent_taps(0, gh[1])
    cotangent_taps(2, gh[0])
    take(5, 0)
    give(5, 0, 1)
    take(3, 1)
    give(3, 1, 7)
    take(5, 1)
    take(3, 0)
    outward(5, 3)
    arrived(xc.at[core, 1], xc_sem.at[core, 1])
    arrived(xc.at[diag, 1], xc_sem.at[diag, 1])
    grad_w = lax.dot_general(xc[:, 1].reshape(128, YX), gp[...], NT, preferred_element_type=F32)
    take(4, 0)
    take(4, 1)
    outward(4)

    pick = lax.broadcasted_iota(jnp.int32, (32, 256), 0)
    source = lax.broadcasted_iota(jnp.int32, (32, 256), 1)
    wanted = pick // 4 * 32 + pick // 2 % 2 * 16 + 2 * z + pick % 2
    r4[col] = jnp.dot(keep(source == wanted), sp[2:10].reshape(256, YX), preferred_element_type=F32).astype(BF)
    others(r4.at[col], r4_sem.at[col])
    hand_over(gc.at[far], gc_sem.at[far])

    for kj in range(8):
        mg[kj % 4, kj // 4] = grad_w[16 * kj:16 * kj + 16, 0:1280]
        ng[kj // 4, kj % 4, :, 0:448] = grad_w[16 * kj:16 * kj + 16, 1280:1728]
        ng[kj // 4, kj % 4, :, 448:512] = jnp.zeros((16, 64), F32)
    arrived(gc.at[core], gc_sem.at[core])
    arrived(gc.at[diag], gc_sem.at[diag])
    gram = lax.dot_general(gc[...].reshape(256, YX), g_ref[...], NT, preferred_element_type=F32)
    for kj in range(8):
        ng[kj // 4, kj % 4, :, 512:576] = gram[32 * kj:32 * kj + 16]
        ng[kj // 4, kj % 4, :, 576:640] = gram[32 * kj + 16:32 * kj + 32]
    send(ng.at[1 - xl], nx, nx_sem.at[0], (((1 - xl) * 4 + yk) * 8 + z, col))
    for step in (1, 2, 3):
        to = (yk + step) % 4
        send(mg.at[to], rg.at[yk], rg_sem.at[yk], ((xl * 4 + to) * 8 + z, col))


    entry = lax.broadcasted_iota(jnp.int32, (128, 864), 0)
    column = lax.broadcasted_iota(jnp.int32, (128, 864), 1)
    home = jnp.where(entry < 96, entry % 32 * 27 + entry // 32 * 9, -27)
    for be in range(9):
        column_ref[be * 128:be * 128 + 128, :] = keep(column == home + be)

    gi[...] = jnp.dot(wg[...], gp[...], preferred_element_type=F32).reshape(4, 32, YX)
    send(gi.at[core], rgi.at[0], gi_sem.at[0], (gz, core))
    send(gi.at[diag], rgi.at[1], gi_sem.at[1], (gz, core))
    hand_over(r4.at[far], r4_sem.at[far])
    for slot, edge in ((0, 0), (1, 0), (10, 7), (11, 7)):
        arrived(sp.at[slot], sp_sem.at[slot, 0])

        @pl.when(k == edge)
        def _():
            sp[slot] = jnp.zeros((32, YX), BF)

    for side in (0, 2):
        xc[col, side] = sp[1 + z + side]
        others(xc.at[col, side], xc_sem.at[col, side])

    arrived(rgi.at[1], gi_sem.at[1])
    up[...] = gi[far] + rgi[1]
    send(up, rgi.at[2], gi_sem.at[2], (gz, far))
    arrived(r4.at[core], r4_sem.at[core])
    arrived(r4.at[diag], r4_sem.at[diag])
    rp[...] = jnp.dot(
        order_ref[...], r4[...].reshape(128, YX), preferred_element_type=F32).astype(BF).reshape(8, 16, YX)

    da[...] = jnp.zeros((784, 128), F32)
    db[...] = jnp.zeros((800, 128), F32)
    edge_plane = jnp.where(k < 4, 0, 7)

    def variants(value, unit, at, size):
        out = []
        for delta in (-2, -1, 0, 1, 2):
            inside = jnp.logical_and(at - delta >= 0, at - delta < size)
            out.append(value if delta == 0 else moved(value, -delta * unit) * keep(inside))
        out.append(value * keep(at >= 1))
        out.append(value * keep(at < size - 1))
        return out

    def factor_plane(v):
        rows = rp[v]
        for tx, line in enumerate(variants(rows, 1, place, SIDE)):
            for ty, plane in enumerate(variants(line, SIDE, row, SIDE)):
                at = (ty * 7 + tx) * 16
                rv[at:at + 16, :] = plane
        beside = sp[pl.ds(v, 5)].reshape(160, YX)
        flag = jnp.where(v == edge_plane, 1.0, 0.0).astype(BF)
        columns = jnp.concatenate([beside, sp[v + 2] * flag], axis=0)
        part = lax.dot_general(rv[...], columns, NT, preferred_element_type=F32)
        da[...] += part[:, 0:128]
        db[0:784, 0:64] += part[:, 128:192]

    @pl.loop(0, 4)
    def _(v):
        factor_plane(v)

    arrived(nx, nx_sem.at[0])
    nt[...] = ng[xl] + nx[...]
    for step in (1, 2, 3):
        to = (yk + step) % 4
        send(nt.at[to], ny.at[yk], ny_sem.at[yk], ((xl * 4 + to) * 8 + z, col))

    @pl.loop(4, 7)
    def _(v):
        factor_plane(v)

    for step in (1, 2, 3):
        slot = (yk + step) % 4
        arrived(rg.at[slot], rg_sem.at[slot])
    mx[1] = mg[yk, 1 - xl] + rg[(yk + 1) % 4, 1 - xl] + rg[(yk + 2) % 4, 1 - xl] + rg[(yk + 3) % 4, 1 - xl]
    send(mx.at[1], rx, rx_sem.at[0], (((1 - xl) * 4 + yk) * 8 + z, col))
    mx[0] = mg[yk, xl] + rg[(yk + 1) % 4, xl] + rg[(yk + 2) % 4, xl] + rg[(yk + 3) % 4, xl]


    @pl.loop(7, 8)
    def _(v):
        factor_plane(v)

    lane = lax.broadcasted_iota(jnp.int32, (25, 128), 1)

    def packed(kj, first):
        out = None
        for q in range(4):
            run = db[pl.ds(2 * kj + q // 2 + 400 * (q % 2), 25, stride=16), :]
            step = (32 * q - first) % 128
            run = pltpu.roll(run, shift=step, axis=1) if step else run
            out = run if out is None else jnp.where(lane // 32 == q, run, out)
        return out

    for kj in range(8):
        for p in range(2):
            mp[kj, 49 * p:49 * p + 49] = da[pl.ds(2 * kj + p, 49, stride=16), :]
        mp[kj, 98:123] = packed(kj, 0)
    for kj in peers:
        send(mp.at[kj], rpf.at[k], rpf_sem.at[k], (kj * 8 + z, col))
    def face_copies(owner):
        return [pltpu.make_async_remote_copy(
            src_ref=me.at[(owner + j) % 8], dst_ref=re.at[owner // 7], send_sem=late_sem.at[24 + j],
            recv_sem=re_sem.at[owner // 7], device_id=((owner + j) % 8 * 8 + z, col),
            device_id_type=MESH) for j in range(1, 8)]

    for owner in (0, 7):
        @pl.when(k == owner)
        def _():
            for kj in range(8):
                me[kj] = packed(kj, 32)
            for copy in face_copies(owner):
                copy.start()
            re[owner // 7] = me[owner]

    arrived(rx, rx_sem.at[0])
    early = mx[0] + rx[...]
    late = nt[yk]
    for step in (1, 2, 3):
        slot = (yk + step) % 4
        arrived(ny.at[slot], ny_sem.at[slot])
        late = late + ny[slot]
    tiles = [early[:, 128 * j:128 * j + 128] for j in range(10)] + [late[:, 128 * j:128 * j + 128] for j in range(5)]
    for j in range(14):
        for zj in range(8):
            b3[zj, 2 * j:2 * j + 2, :] = tiles[j][2 * zj:2 * zj + 2]
    sides = (tiles[14], pltpu.roll(tiles[14], shift=64, axis=1))
    for zj in range(8):
        b3[zj, 28:32, :] = sides[zj // 4][4 * (zj % 4):4 * (zj % 4) + 4]
    for zj in ring:
        send(b3.at[zj], rb.at[z], rb_sem.at[z], (k * 8 + zj, col))

    for side in (0, 2):
        hand_over(xc.at[far, side], xc_sem.at[far, side])

    for side in (0, 2):
        arrived(xc.at[core, side], xc_sem.at[core, side])
        arrived(xc.at[diag, side], xc_sem.at[diag, side])

    for a in range(3):
        plane = xc[:, a].reshape(128, YX)
        for e in range(3):
            line = shifted(plane, 0, e - 1)
            for b in range(3):
                tap = 9 * a + 3 * b + e
                xp[tap * 128:(tap + 1) * 128, :] = shifted(line, b - 1, 0)
    y_ref[0] = jnp.dot(wy[...], xp[...], preferred_element_type=F32).astype(BF)

    arrived(rgi.at[0], gi_sem.at[0])
    arrived(rgi.at[2], gi_sem.at[2])
    gi_ref[0] = (gi[col] + rgi[0] + rgi[2]).astype(BF)

    total = mp[k]
    for kj in peers:
        arrived(rpf.at[kj], rpf_sem.at[kj])
        total = total + rpf[kj]
    for owner in (0, 7):
        @pl.when(k != owner)
        def _():
            arrived(re.at[owner // 7], re_sem.at[owner // 7])
    low, high = re[0], re[1]
    pad = jnp.zeros((49, 32), F32)

    def unpacked(value, p):
        at = 64 * p
        return jnp.concatenate([value[0:25, at:at + 32], value[0:24, at + 32:at + 64]], axis=0)

    for p in range(2):
        head = total[49 * p:49 * p + 49]
        m2, m1, zero, p1 = [head[:, 32 * i:32 * i + 32] for i in range(4)]
        p2 = unpacked(total[98:123], p)
        first, last = unpacked(low, p), unpacked(high, p)
        wide = jnp.concatenate(
            [zero - last, p1, p2, pad, m1, zero, p1, pad, m2, m1, zero - first, pad], axis=1)
        for part in range(3):
            piece = wide.astype(BF)
            wide = wide - piece.astype(F32)
            picked = jnp.dot(choice_ref[...], piece, preferred_element_type=F32).astype(BF)
            for a in range(3):
                at = (part * 6 + p * 3 + a) * 16
                for be in range(9):
                    lh[at:at + 16, be * 128:be * 128 + 128] = picked[be * 16:be * 16 + 16, a * 128:a * 128 + 128]
    factor = jnp.dot(lh[...], column_ref[...], preferred_element_type=F32)
    factor = (factor[0:96] + factor[96:192] + factor[192:288]) * (1.0 / 65536)
    for block in range(6):
        pf_ref[block * 9:block * 9 + 9, :] = factor[block * 16:block * 16 + 9]

    total = b3[z]
    for zj in ring:
        arrived(rb.at[zj], rb_sem.at[zj])
        total = total + rb[zj]
    gf_ref[...] = total[28:32, 0:64] * (1.0 / 65536)
    for tap in range(TAPS):
        for p in range(2):
            at = 2 * (tap // 2) + p
            gw_ref[p * 27 + tap:p * 27 + tap + 1, :] = total[at:at + 1, 64 * (tap % 2):64 * (tap % 2) + 64] * (1.0 / 256)

    for _, copy in x_edges:
        copy.wait_send()
    for copy in sends:
        copy.wait_send()
    for owner in (0, 7):
        @pl.when(k == owner)
        def _():
            for copy in face_copies(owner):
                copy.wait_send()


def deliver(*refs):
    for i in range(5):
        refs[5 + i][...] = refs[i][...]


def shards(x_field, weights, grad_out):
    vmem = pl.BlockSpec(memory_space=pltpu.VMEM)
    there = pl.BlockSpec(memory_space=pl.ANY)
    dma = pltpu.SemaphoreType.DMA
    shapes = (
        jax.ShapeDtypeStruct((1, 64, YX), BF),
        jax.ShapeDtypeStruct((1, 32, YX), BF),
        jax.ShapeDtypeStruct((54, 64), F32),
        jax.ShapeDtypeStruct((54, 864), F32),
        jax.ShapeDtypeStruct((4, 64), F32),
    )
    results = pl.pallas_call(
        kernel,
        out_shape=shapes,
        in_specs=[there] * 5,
        out_specs=(vmem,) * 5,
        scratch_shapes=[
            pltpu.VMEM((64, YX), BF),
            pltpu.VMEM((64, 3456), BF),
            pltpu.VMEM((128, 128), BF),
            pltpu.VMEM((144, 49), BF),
            pltpu.VMEM((1152, 864), BF),
            pltpu.VMEM((3456, 128), F32),
            pltpu.VMEM((64, 3456), BF),
            pltpu.VMEM((128, 1728), BF),
            pltpu.VMEM((4, 3, 32, YX), BF),
            pltpu.VMEM((4, 64, YX), BF),
            pltpu.VMEM((2, 64, YX), BF),
            pltpu.VMEM((12, 32, YX), BF),
            pltpu.VMEM((4, 32, YX), BF),
            pltpu.VMEM((8, 16, YX), BF),
            pltpu.VMEM((3456, YX), BF),
            pltpu.VMEM((1728, YX), BF),
            pltpu.VMEM((784, YX), BF),
            pltpu.VMEM((784, 128), F32),
            pltpu.VMEM((800, 128), F32),
            pltpu.VMEM((4, 2, 16, 1280), F32),
            pltpu.VMEM((4, 2, 16, 1280), F32),
            pltpu.VMEM((2, 16, 1280), F32),
            pltpu.VMEM((16, 1280), F32),
            pltpu.VMEM((2, 4, 16, 640), F32),
            pltpu.VMEM((4, 16, 640), F32),
            pltpu.VMEM((4, 16, 640), F32),
            pltpu.VMEM((4, 16, 640), F32),
            pltpu.VMEM((8, 32, 128), F32),
            pltpu.VMEM((8, 32, 128), F32),
            pltpu.VMEM((8, 123, 128), F32),
            pltpu.VMEM((8, 123, 128), F32),
            pltpu.VMEM((8, 25, 128), F32),
            pltpu.VMEM((2, 25, 128), F32),
            pltpu.VMEM((4, 32, YX), F32),
            pltpu.VMEM((3, 32, YX), F32),
            pltpu.VMEM((32, YX), F32),
            pltpu.VMEM((288, 1152), BF),
            dma((72,)),
            dma((32,)),
            dma((8,)),
            dma((4, 3)),
            dma((4,)),
            dma((2,)),
            dma((12, 2)),
            dma((4,)),
            dma((4,)),
            dma((1,)),
            dma((1,)),
            dma((4,)),
            dma((8,)),
            dma((8,)),
            dma((2,)),
            dma((3,)),
        ],
        compiler_params=pltpu.CompilerParams(
            collective_id=0, has_side_effects=True, vmem_limit_bytes=56 * 2**20),
    )(x_field, grad_out, weights,
      jnp.asarray(channel_order(), BF), jnp.asarray(type_choice(), BF))
    return pl.pallas_call(
        deliver,
        out_shape=shapes,
        in_specs=[vmem] * 5,
        out_specs=(vmem,) * 5,
    )(*results)


def solution(mesh):
    return jax.shard_map(
        shards,
        mesh=mesh,
        in_specs=(P("gz", "col", None), P("col", None), P("gz", "col", None)),
        out_specs=(
            P("gz", "col", None),
            P("gz", "col", None),
            P("gz", "col"),
            P("gz", "col"),
            P("gz", "col"),
        ),
        check_vma=False,
    )
```
